32 devices in a mesh: expert: 8 (over z, y), tensor: 4 (over x, core).
Axes of the slice: x: 2, y: 2, z: 4, core: 2. Of those that a mesh axis runs over, the one named last changes fastest.
Arguments:
- tokens: bfloat16 [2048, 2560], P('expert', 'tensor'), may hold values from -6 to 6
- route_logit: float32 [2048], P('expert'), may hold values from -6 to 6
- expert_ids: int32 [2048, 1], P('expert'), may hold values from 0 to 7; in each aligned block of 256 rows (0 to 255, 256 to 511, ...) at most 40 rows name the same one
- w_gate: bfloat16 [8, 2560, 4096], P('expert', None, 'tensor'), may hold values from -0.125 to 0.125
- w_up: bfloat16 [8, 2560, 4096], P('expert', None, 'tensor'), may hold values from -0.125 to 0.125
- w_down: bfloat16 [8, 4096, 2560], P('expert', 'tensor'), may hold values from -0.09375 to 0.09375
Outputs:
- mixed: bfloat16 [2048, 2560], P('expert', 'tensor')
The draws below stay inside these ranges and needn't reach their ends.
Inputs may be any that keep to these rules, and one draw needn't show every extreme that they name: `expert_ids`: in each aligned block of 256 tokens no expert id appears more than 40 times, and in some block one expert appears exactly 40 times.
All inputs are finite; a program needn't handle non-finite values.
Results may differ from the reference program's by a relative error of at most 0.0065.
Values may be sent and summed in bfloat16 or wider, within the bound.
A program may use at most 64 MiB of HBM per device.

```python
import math
import jax
import jax.numpy as jnp
import numpy as np
from jax import lax

D = 2560
FF = 4096
TOK_G = 256
EXPERTS = 8
CAP = 40
TOKENS = 2048
N_EXPERT = 8


def block_scale(key, shape, pieces, low, high):
    def one(axis_at, blocks):
        heights = jax.random.uniform(jax.random.fold_in(jax.random.fold_in(key, 6), axis_at), (blocks,), jnp.float32, low / len(pieces), high / len(pieces))
        return jnp.repeat(jnp.exp(heights), shape[axis_at] // blocks).reshape((-1,) + (1,) * (len(shape) - axis_at - 1))

    loudness = one(*pieces[0])
    for cut in pieces[1:]:
        loudness = loudness * one(*cut)
    return loudness


def assign_block(stream_key, own, number, rows, amount, top, most, lean):
    ranking = jax.random.permutation(stream_key, amount)
    crowded, common = load_shares(amount, rows * top, most, lean, True), load_shares(amount, rows * top, most, lean, False)
    places = jnp.arange(amount)

    def named(tallies, offset_by):
        used = int((tallies > 0).sum())
        fixed = max(1, used // 4)
        shifted = fixed + (places - fixed + offset_by * (used - fixed)) % max(1, amount - fixed)
        return jnp.zeros((amount,), jnp.int32).at[ranking[jnp.where(places < fixed, places, shifted)]].set(jnp.asarray(tallies, jnp.int32))

    tallies = jnp.where(number % 4 == 0, named(crowded, number // 4), named(common, number - number // 4 - 1))
    mixed = jax.random.permutation(jax.random.fold_in(own, 3), amount)
    donor, sink = mixed[0:amount // 2 * 2:2], mixed[1:amount // 2 * 2:2]
    room = jnp.minimum(tallies[donor] - 1, most - tallies[sink]) // 2
    room = jnp.where((donor == ranking[0]) | (sink == ranking[0]) | (tallies[sink] == 0), 0, jnp.maximum(room, 0))
    shifted = jax.random.randint(jax.random.fold_in(own, 4), (amount // 2,), 0, 1 << 20) % (room + 1)
    tallies = tallies.at[donor].add(-shifted).at[sink].add(shifted)
    labels = jnp.searchsorted(jnp.cumsum(tallies), jnp.arange(rows * top), side="right").astype(jnp.int32)
    table = labels.reshape(top, rows).T
    table = table[jax.random.permutation(jax.random.fold_in(own, 1), rows)]
    offset_by = jax.random.randint(jax.random.fold_in(own, 2), (rows, 1), 0, top)
    return jnp.take_along_axis(table, (jnp.arange(top)[None, :] + offset_by) % top, axis=1)


def load_shares(amount, total, most, slope, full):
    loads = [(1 << 20) // math.isqrt(standing ** slope) + 1 for standing in range(1, amount + 1)]
    largest = most if full else min(most, max(-(-total // amount), total * loads[0] // sum(loads)))
    least = 1 if total - largest >= amount - 1 else 0
    given, spare = [largest] + [least] * (amount - 1), total - largest - least * (amount - 1)
    while spare > 0:
        candidates = [i for i in range(1, amount) if given[i] < largest] or [i for i in range(1, amount) if given[i] < most]
        whole, remaining = sum([loads[i] for i in candidates]), spare
        for i in candidates:
            extra = min(most - given[i], max(1, remaining * loads[i] // whole), spare)
            given[i] = given[i] + extra
            spare = spare - extra
    return np.array(given)


def bell_draw(key, extent, scale, most, cuts=(), kind=jnp.bfloat16):
    entries = jax.random.normal(key, extent, jnp.float32) * scale
    if len(cuts) > 0:
        entries = block_scale(key, extent, cuts, -0.22, 0.18) * entries
    return jnp.clip(entries, min=-most, max=most).astype(kind)


def setup_inputs(seed: int = 0) -> dict:
    streams_of = jax.random.split(jax.random.key(seed), 7)
    tokens = bell_draw(streams_of[0], (TOKENS, D), 1.0, 6.0, ((0, 8), (1, 4)))
    route_logit = bell_draw(streams_of[1], (TOKENS,), 1.5, 6.0, ((0, 8),), jnp.float32)
    expert_ids_keys = jax.random.split(jax.random.fold_in(streams_of[2], 1), TOKENS // TOK_G)
    expert_ids_turns = jax.random.permutation(jax.random.fold_in(streams_of[2], 3), TOKENS // TOK_G)
    expert_ids = jax.vmap(lambda own, number: assign_block(jax.random.fold_in(streams_of[2], 2), own, number, TOK_G, EXPERTS, 1, CAP, 2))(expert_ids_keys, expert_ids_turns).reshape((TOKENS, 1))
    w_gate = bell_draw(streams_of[3], (EXPERTS, D, FF), D ** -0.5, 0.125, ((0, 8), (2, 4)))
    w_up = bell_draw(streams_of[4], (EXPERTS, D, FF), D ** -0.5, 0.125, ((0, 8), (2, 4)))
    w_down = bell_draw(streams_of[5], (EXPERTS, FF, D), FF ** -0.5, 0.09375, ((0, 8), (1, 4)))
    return dict(tokens=tokens, route_logit=route_logit, expert_ids=expert_ids, w_gate=w_gate, w_up=w_up, w_down=w_down)


def expert_ffn(items):
    rows, gate_w, up_w, down_w = items
    rows_f = rows.astype(jnp.float32)
    gate_val = jnp.dot(rows_f, gate_w.astype(jnp.float32), precision=lax.Precision.HIGHEST)
    lift_val = jnp.dot(rows_f, up_w.astype(jnp.float32), precision=lax.Precision.HIGHEST)
    hidden = (jax.nn.silu(gate_val) * lift_val).astype(jnp.bfloat16)
    result = jnp.dot(hidden.astype(jnp.float32), down_w.astype(jnp.float32), precision=lax.Precision.HIGHEST)
    return result.astype(jnp.bfloat16)


def reference(tokens, route_logit, expert_ids, w_gate, w_up, w_down):
    route = expert_ids[:, 0].astype(jnp.int32)
    factor = jax.nn.sigmoid(route_logit.astype(jnp.float32))
    scaled = (factor[:, None] * tokens.astype(jnp.float32)).astype(jnp.bfloat16)
    one_hot = (route[:, None] == jnp.arange(EXPERTS, dtype=jnp.int32)[None, :]).astype(jnp.int32)
    blocked = one_hot.reshape(N_EXPERT, TOK_G, EXPERTS)
    earlier = jnp.cumsum(blocked, axis=1) - blocked
    position = jnp.sum(earlier * blocked, axis=2).reshape(TOKENS).astype(jnp.int32)
    block_index = (jnp.arange(TOKENS, dtype=jnp.int32) // TOK_G).astype(jnp.int32)
    row_index = (block_index * CAP + position).astype(jnp.int32)
    buffer = jnp.zeros((EXPERTS, N_EXPERT * CAP, D), jnp.bfloat16).at[route, row_index].set(scaled)
    outputs = lax.map(expert_ffn, (buffer, w_gate, w_up, w_down))
    return outputs[route, row_index]
```

```python
import functools

import jax
import jax.numpy as jnp
from jax import lax
from jax.experimental import pallas as pl
from jax.experimental.pallas import tpu as pltpu
from jax.sharding import PartitionSpec as P

MESH = pl.DeviceIdType.MESH
F32 = jnp.float32
BF16 = jnp.bfloat16


def plan(width, cap):
    chunks, off, row = [], 0, 0
    while off < width:
        lanes = min(256, width - off)
        rows = -(-(cap * (lanes // 128)) // 16) * 16
        chunks.append((off, lanes, row, rows))
        off, row = off + lanes, row + rows
    return chunks, row


def pack(block, lanes, rows):
    parts = [block[:, i : i + 128] for i in range(0, lanes, 128)]
    spare = rows - block.shape[0] * len(parts)
    if spare:
        parts.append(jnp.zeros((spare, 128), F32))
    return jnp.concatenate(parts, axis=0) if len(parts) > 1 else parts[0]


def unpack(packed, lanes, cap):
    packed = packed.astype(F32)
    parts = [packed[i * cap : (i + 1) * cap] for i in range(lanes // 128)]
    return jnp.concatenate(parts, axis=1) if len(parts) > 1 else parts[0]


def kernel(
    n_exp, n_ten, cap, chunks,
    tokens, logit, ids, w_gate, w_up, w_down,
    out,
    wg, wu, wd, send_d, recv_d, send_r, recv_r, x, acc_g, acc_u, hidden, combine,
    far_out, far_in, near_out, near_in, near_own, half_out, half_in,
    w_sem, ds_sem, dr_sem, rs_sem, rr_sem, sib_s, sib_r, x_s, x_r, fw_s, fw_r,
    far_s, far_r, near_s, near_r, half_s, half_r,
):
    g = lax.axis_index("expert")
    t = lax.axis_index("tensor")
    sib = t + 1 - 2 * lax.rem(t, 2)
    across = lax.rem(t + 2, 4)
    diag = lax.rem(sib + 2, 4)
    tok, width = tokens.shape
    slots = n_exp * cap
    n_ff = wg.shape[2]
    order = list(range(1, n_exp))

    loads = []
    for s in range(n_ten):
        loads.append(pltpu.make_async_copy(w_gate.at[0, pl.ds(s * width, width)], wg.at[s], w_sem.at[0, s]))
        loads.append(pltpu.make_async_copy(w_up.at[0, pl.ds(s * width, width)], wu.at[s], w_sem.at[1, s]))
    for s in range(n_ten):
        loads.append(
            pltpu.make_async_copy(w_down.at[0, :, pl.ds(s * width, width)], wd.at[s], w_sem.at[2, s])
        )
    for load in loads:
        load.start()

    barrier = pltpu.get_barrier_semaphore()
    for k in order:
        pl.semaphore_signal(barrier, inc=1, device_id=(lax.rem(g + k, n_exp), t), device_id_type=MESH)
    for peer in (sib, across):
        pl.semaphore_signal(barrier, inc=1, device_id=(g, peer), device_id_type=MESH)

    ids_row = ids[...]
    one_hot = lax.broadcasted_iota(jnp.int32, (n_exp, tok), 0) == ids_row
    older = lax.broadcasted_iota(jnp.int32, (tok, tok), 0)
    newer = lax.broadcasted_iota(jnp.int32, (tok, tok), 1)
    before = jnp.where(older < newer, 1.0, 0.0).astype(BF16)
    hot = jnp.where(one_hot, 1.0, 0.0)
    earlier = jnp.dot(hot.astype(BF16), before, preferred_element_type=F32)
    position = jnp.sum(earlier * hot, axis=0, keepdims=True)
    dest = ids_row.astype(F32) * float(cap) + position
    eye = older == newer
    dest_col = jnp.sum(jnp.where(eye, dest, 0.0), axis=1, keepdims=True)
    slot_row = lax.broadcasted_iota(jnp.int32, (slots, tok), 0).astype(F32)
    dispatch = jnp.where(slot_row == dest, 1.0, 0.0).astype(BF16)
    slot_col = lax.broadcasted_iota(jnp.int32, (tok, slots), 1).astype(F32)
    combine[...] = jnp.where(slot_col == dest_col, 1.0, 0.0).astype(BF16)
    factor = jnp.sum(jnp.where(eye, jax.nn.sigmoid(logit[...]), 0.0), axis=1, keepdims=True)

    def exchange(c, src, dst, s_sem, r_sem):
        _, _, row, rows = chunks[c]
        copies = []
        for k in order:
            e = lax.rem(g + k, n_exp)
            copies.append(
                pltpu.make_async_remote_copy(
                    src_ref=src.at[e, pl.ds(row, rows)],
                    dst_ref=dst.at[g, pl.ds(row, rows)],
                    send_sem=s_sem.at[k, c],
                    recv_sem=r_sem.at[k, c],
                    device_id=(e, t),
                    device_id_type=MESH,
                )
            )
        return copies

    def to_tensor(src, dst, s_sem, r_sem, peer):
        return pltpu.make_async_remote_copy(
            src_ref=src, dst_ref=dst, send_sem=s_sem, recv_sem=r_sem, device_id=(g, peer), device_id_type=MESH
        )

    sends = []
    dispatches = []
    for c, (off, lanes, row, rows) in enumerate(chunks):
        scaled = (factor * tokens[:, off : off + lanes].astype(F32)).astype(BF16)
        outgoing = jnp.dot(dispatch, scaled, preferred_element_type=F32)
        for e in range(n_exp):
            send_d[e, row : row + rows] = pack(outgoing[e * cap : (e + 1) * cap], lanes, rows).astype(BF16)
        if c == 0:
            pl.semaphore_wait(barrier, n_exp - 1 + 2)
        copies = exchange(c, send_d, recv_d, ds_sem, dr_sem)
        for copy in copies:
            copy.start()
        recv_d[g, row : row + rows] = send_d[g, row : row + rows]
        dispatches.append(copies)
        sends += copies

    crossing, sides = [], []
    for c, (off, lanes, row, rows) in enumerate(chunks):
        for copy in dispatches[c]:
            copy.wait_recv()
        x[t, :, off : off + lanes] = jnp.concatenate(
            [unpack(recv_d[e, row : row + rows], lanes, cap) for e in range(n_exp)], axis=0
        ).astype(BF16)
        part = x.at[t, :, pl.ds(off, lanes)]
        crossing.append(to_tensor(part, part, x_s.at[c], x_r.at[c], across))
        sides.append(to_tensor(part, part, sib_s.at[c], sib_r.at[c], sib))
        crossing[-1].start()
        sides[-1].start()
    sends += crossing + sides

    forwards = []

    def forward(c):
        off, lanes, _, _ = chunks[c]
        crossing[c].wait_recv()
        part = x.at[across, :, pl.ds(off, lanes)]
        forwards.append(to_tensor(part, part, fw_s.at[c], fw_r.at[c], sib))
        forwards[-1].start()

    def project(s, first, last):
        @pl.loop(0, n_ff // 256)
        def _(n):
            cols = pl.ds(pl.multiple_of(n * 256, 256), 256)
            rows_in = x[s]
            gate = jnp.dot(rows_in, wg[s, :, cols], preferred_element_type=F32)
            lift = jnp.dot(rows_in, wu[s, :, cols], preferred_element_type=F32)
            if not first:
                gate = gate + acc_g[:, cols]
                lift = lift + acc_u[:, cols]
            if last:
                hidden[:, cols] = (jax.nn.silu(gate) * lift).astype(BF16)
            else:
                acc_g[:, cols] = gate
                acc_u[:, cols] = lift

    for load in loads:
        load.wait()
    n_chunks = len(chunks)
    forward(0)
    project(t, True, False)
    for c in range(1, n_chunks - 1):
        forward(c)
    for copy in sides:
        copy.wait_recv()
    project(sib, False, False)
    forward(n_chunks - 1)
    project(across, False, False)
    for copy in forwards:
        copy.wait_recv()
    project(diag, False, True)
    sends += forwards

    def partial(s, c):
        off, lanes, _, _ = chunks[c]
        return jnp.dot(hidden[...], wd[s, :, off : off + lanes], preferred_element_type=F32)

    halves = []

    def half(c, copy, mine):
        off, lanes, _, _ = chunks[c]
        copy.wait_recv()
        half_out[:, off : off + lanes] = (mine + far_in[:, off : off + lanes]).astype(BF16)
        halves.append(
            to_tensor(
                half_out.at[:, pl.ds(off, lanes)], half_in.at[:, pl.ds(off, lanes)],
                half_s.at[c], half_r.at[c], across,
            )
        )
        halves[-1].start()
        sends.append(halves[-1])

    for c, (off, lanes, _, _) in enumerate(chunks):
        far_out[:, off : off + lanes] = partial(diag, c)
        copy = to_tensor(
            far_out.at[:, pl.ds(off, lanes)], far_in.at[:, pl.ds(off, lanes)], far_s.at[c], far_r.at[c], sib
        )
        copy.start()
        sends.append(copy)
        half(c, copy, partial(across, c))

    nears = []
    for c, (off, lanes, _, _) in enumerate(chunks):
        near_out[:, off : off + lanes] = partial(sib, c)
        copy = to_tensor(
            near_out.at[:, pl.ds(off, lanes)], near_in.at[:, pl.ds(off, lanes)], near_s.at[c], near_r.at[c], sib
        )
        copy.start()
        nears.append(copy)
        near_own[:, off : off + lanes] = partial(t, c)
    sends += nears

    returns = []
    for c, (off, lanes, row, rows) in enumerate(chunks):
        nears[c].wait_recv()
        halves[c].wait_recv()
        total = (
            near_own[:, off : off + lanes] + near_in[:, off : off + lanes] + half_in[:, off : off + lanes].astype(F32)
        )
        for e in range(n_exp):
            send_r[e, row : row + rows] = pack(total[e * cap : (e + 1) * cap], lanes, rows).astype(BF16)
        copies = exchange(c, send_r, recv_r, rs_sem, rr_sem)
        for copy in copies:
            copy.start()
        recv_r[g, row : row + rows] = send_r[g, row : row + rows]
        returns.append(copies)
        sends += copies

    for c, (off, lanes, row, rows) in enumerate(chunks):
        for copy in returns[c]:
            copy.wait_recv()
        returned = jnp.concatenate(
            [unpack(recv_r[e, row : row + rows], lanes, cap) for e in range(n_exp)], axis=0
        ).astype(BF16)
        out[:, off : off + lanes] = jnp.dot(combine[...], returned, preferred_element_type=F32).astype(BF16)

    for copy in sends:
        copy.wait_send()


def fused(tokens, route_logit, expert_ids, w_gate, w_up, w_down):
    n_exp = lax.axis_size("expert")
    n_ten = lax.axis_size("tensor")
    tok, width = tokens.shape
    n_ff = w_gate.shape[2]
    cap = 5 * tok // (4 * n_exp)
    slots = n_exp * cap
    chunks, block_rows = plan(width, cap)
    n_c = len(chunks)
    dma = pltpu.SemaphoreType.DMA
    vmem = pltpu.VMEM
    blocks = (n_exp, block_rows, 128)
    return pl.pallas_call(
        functools.partial(kernel, n_exp, n_ten, cap, chunks),
        out_shape=jax.ShapeDtypeStruct((tok, width), BF16),
        in_specs=[pl.BlockSpec(memory_space=vmem)] * 3 + [pl.BlockSpec(memory_space=pl.ANY)] * 3,
        out_specs=pl.BlockSpec(memory_space=vmem),
        scratch_shapes=[
            vmem((n_ten, width, n_ff), BF16),
            vmem((n_ten, width, n_ff), BF16),
            vmem((n_ten, n_ff, width), BF16),
            vmem(blocks, BF16),
            vmem(blocks, BF16),
            vmem(blocks, BF16),
            vmem(blocks, BF16),
            vmem((n_ten, slots, width), BF16),
            vmem((slots, n_ff), F32),
            vmem((slots, n_ff), F32),
            vmem((slots, n_ff), BF16),
            vmem((tok, slots), BF16),
            vmem((slots, width), F32),
            vmem((slots, width), F32),
            vmem((slots, width), F32),
            vmem((slots, width), F32),
            vmem((slots, width), F32),
            vmem((slots, width), BF16),
            vmem((slots, width), BF16),
            dma((3, n_ten)),
        ]
        + [dma((n_exp, n_c))] * 4
        + [dma((n_c,))] * 12,
        compiler_params=pltpu.CompilerParams(
            collective_id=0, has_side_effects=True, vmem_limit_bytes=48 * 1024 * 1024
        ),
        cost_estimate=pl.CostEstimate(
            flops=6 * slots * n_ten * width * n_ff,
            bytes_accessed=6 * n_ten * width * n_ff,
            transcendentals=slots * n_ff,
        ),
    )(tokens, route_logit.reshape(1, tok), expert_ids.reshape(1, tok), w_gate, w_up, w_down)


def on_device(tokens, route_logit, expert_ids, w_gate, w_up, w_down):
    expert_count = lax.axis_size("expert")
    tok_rows, width_local = tokens.shape
    capacity = 5 * tok_rows // (4 * expert_count)
    if (
        lax.axis_size("tensor") == 4
        and capacity % 8 == 0
        and width_local % 128 == 0
        and w_gate.shape[2] % 256 == 0
        and expert_count <= 8
    ):
        return fused(tokens, route_logit, expert_ids, w_gate, w_up, w_down)
    slot_count = expert_count * capacity
    route = expert_ids[:, 0]
    one_hot = (route[:, None] == jnp.arange(expert_count, dtype=jnp.int32)[None, :]).astype(
        jnp.int32
    )
    earlier = jnp.cumsum(one_hot, axis=0) - one_hot
    position = jnp.sum(earlier * one_hot, axis=1)
    destination = route * capacity + position
    dispatch_map = (
        jnp.arange(slot_count, dtype=jnp.int32)[:, None] == destination[None, :]
    ).astype(jnp.bfloat16)
    factor = jax.nn.sigmoid(route_logit)
    scaled = (factor[:, None] * tokens.astype(jnp.float32)).astype(jnp.bfloat16)
    outgoing = jnp.dot(dispatch_map, scaled, preferred_element_type=jnp.float32).astype(
        jnp.bfloat16
    )
    outgoing = outgoing.reshape(expert_count, capacity, width_local)
    arrived = lax.all_to_all(outgoing, "expert", split_axis=0, concat_axis=0, tiled=True).reshape(
        slot_count, width_local
    )
    gate_local = w_gate[0]
    lift_local = w_up[0]
    down_local = w_down[0]
    piece = lax.all_gather(arrived, "tensor", axis=1, tiled=True)
    gate_val = jnp.dot(piece, gate_local, preferred_element_type=jnp.float32)
    lift_val = jnp.dot(piece, lift_local, preferred_element_type=jnp.float32)
    hidden = (jax.nn.silu(gate_val) * lift_val).astype(jnp.bfloat16)
    summed = lax.psum_scatter(
        lax.dot_general(
            down_local, hidden, (((0,), (1,)), ((), ())), preferred_element_type=jnp.float32
        ),
        "tensor",
        scatter_dimension=0,
        tiled=True,
    )
    expert_out = summed.astype(jnp.bfloat16).reshape(width_local, expert_count, capacity)
    returned = lax.all_to_all(
        expert_out, "expert", split_axis=1, concat_axis=1, tiled=True
    ).reshape(width_local, slot_count)
    mixed = lax.dot_general(
        dispatch_map, returned, (((0,), (1,)), ((), ())), preferred_element_type=jnp.float32
    )
    return mixed.astype(jnp.bfloat16)


def solution(mesh):
    return jax.shard_map(
        on_device,
        mesh=mesh,
        in_specs=(
            P("expert", "tensor"),
            P("expert"),
            P("expert", None),
            P("expert", None, "tensor"),
            P("expert", None, "tensor"),
            P("expert", "tensor", None),
        ),
        out_specs=P("expert", "tensor"),
        check_vma=False,
    )
```

```python
import functools

import jax
import jax.numpy as jnp
from jax import lax
from jax.experimental import pallas as pl
from jax.experimental.pallas import tpu as pltpu
from jax.sharding import PartitionSpec as P

MESH = pl.DeviceIdType.MESH
LIMIT = 63 * 1024 * 1024
F32 = jnp.float32
BF16 = jnp.bfloat16


def plan(width, cap):
    chunks, off, row = [], 0, 0
    while off < width:
        lanes = min(256, width - off)
        rows = -(-(cap * (lanes // 128)) // 16) * 16
        chunks.append((off, lanes, row, rows))
        off, row = off + lanes, row + rows
    return chunks, row


def pack(block, lanes, rows):
    parts = [block[:, i : i + 128] for i in range(0, lanes, 128)]
    spare = rows - block.shape[0] * len(parts)
    if spare:
        parts.append(jnp.zeros((spare, 128), F32))
    return jnp.concatenate(parts, axis=0) if len(parts) > 1 else parts[0]


def unpack(packed, lanes, cap):
    packed = packed.astype(F32)
    parts = [packed[i * cap : (i + 1) * cap] for i in range(lanes // 128)]
    return jnp.concatenate(parts, axis=1) if len(parts) > 1 else parts[0]


def kernel(
    n_exp, n_ten, cap, chunks,
    tokens_in, logit_in, ids_in, w_gate, w_up, w_down,
    out,
    tokens, logit, ids, wg, wu, wd, send_d, recv_d, send_r, recv_r, x, acc_g, acc_u, hidden, combine,
    far_out, far_in, far_own, near_out, near_in, near_own, half_out, half_in,
    in_sem, w_sem, ds_sem, dr_sem, rs_sem, rr_sem, sib_s, sib_r, x_s, x_r, fw_s, fw_r,
    far_s, far_r, near_s, near_r, half_s, half_r,
):
    g = lax.axis_index("expert")
    t = lax.axis_index("tensor")
    sib = t + 1 - 2 * lax.rem(t, 2)
    across = lax.rem(t + 2, 4)
    diag = lax.rem(sib + 2, 4)
    tok, width = tokens.shape
    slots = n_exp * cap
    n_ff = wg.shape[2]
    order = list(range(1, n_exp))

    small = [
        pltpu.make_async_copy(src, dst, in_sem.at[i])
        for i, (src, dst) in enumerate(((ids_in, ids), (logit_in, logit), (tokens_in, tokens)))
    ]
    for copy in small:
        copy.start()

    barrier = pltpu.get_barrier_semaphore()
    for k in order:
        pl.semaphore_signal(barrier, inc=1, device_id=(lax.rem(g + k, n_exp), t), device_id_type=MESH)
    for peer in (sib, across):
        pl.semaphore_signal(barrier, inc=1, device_id=(g, peer), device_id_type=MESH)

    small[0].wait()
    ids_row = ids[...]
    one_hot = lax.broadcasted_iota(jnp.int32, (n_exp, tok), 0) == ids_row
    older = lax.broadcasted_iota(jnp.int32, (tok, tok), 0)
    newer = lax.broadcasted_iota(jnp.int32, (tok, tok), 1)
    before = jnp.where(older < newer, 1.0, 0.0).astype(BF16)
    hot = jnp.where(one_hot, 1.0, 0.0)
    earlier = jnp.dot(hot.astype(BF16), before, preferred_element_type=F32)
    position = jnp.sum(earlier * hot, axis=0, keepdims=True)
    dest = ids_row.astype(F32) * float(cap) + position
    eye = older == newer
    slot_row = lax.broadcasted_iota(jnp.int32, (slots, tok), 0).astype(F32)
    dispatch = jnp.where(slot_row == dest, 1.0, 0.0).astype(BF16)
    small[1].wait()
    factor = jnp.sum(jnp.where(eye, jax.nn.sigmoid(logit[...]), 0.0), axis=1, keepdims=True)

    def exchange(c, src, dst, s_sem, r_sem):
        _, _, row, rows = chunks[c]
        copies = []
        for k in order:
            e = lax.rem(g + k, n_exp)
            copies.append(
                pltpu.make_async_remote_copy(
                    src_ref=src.at[e, pl.ds(row, rows)],
                    dst_ref=dst.at[g, pl.ds(row, rows)],
                    send_sem=s_sem.at[k, c],
                    recv_sem=r_sem.at[k, c],
                    device_id=(e, t),
                    device_id_type=MESH,
                )
            )
        return copies

    def to_tensor(src, dst, s_sem, r_sem, peer):
        return pltpu.make_async_remote_copy(
            src_ref=src, dst_ref=dst, send_sem=s_sem, recv_sem=r_sem, device_id=(g, peer), device_id_type=MESH
        )

    small[2].wait()
    sends = []
    dispatches = []
    for c, (off, lanes, row, rows) in enumerate(chunks):
        scaled = (factor * tokens[:, off : off + lanes].astype(F32)).astype(BF16)
        outgoing = jnp.dot(dispatch, scaled, preferred_element_type=F32)
        for e in range(n_exp):
            send_d[e, row : row + rows] = pack(outgoing[e * cap : (e + 1) * cap], lanes, rows).astype(BF16)
        if c == 0:
            pl.semaphore_wait(barrier, n_exp - 1 + 2)
        copies = exchange(c, send_d, recv_d, ds_sem, dr_sem)
        for copy in copies:
            copy.start()
        recv_d[g, row : row + rows] = send_d[g, row : row + rows]
        dispatches.append(copies)
        sends += copies

    loads = []
    for s in range(n_ten):
        loads.append(pltpu.make_async_copy(w_gate.at[0, pl.ds(s * width, width)], wg.at[s], w_sem.at[0, s]))
        loads.append(pltpu.make_async_copy(w_up.at[0, pl.ds(s * width, width)], wu.at[s], w_sem.at[1, s]))
    for s in range(n_ten):
        loads.append(
            pltpu.make_async_copy(w_down.at[0, :, pl.ds(s * width, width)], wd.at[s], w_sem.at[2, s])
        )
    for load in loads:
        load.start()
    gate_loads, down_loads = loads[: 2 * n_ten], loads[2 * n_ten :]

    dest_col = jnp.sum(jnp.where(eye, dest, 0.0), axis=1, keepdims=True)
    slot_col = lax.broadcasted_iota(jnp.int32, (tok, slots), 1).astype(F32)
    combine[...] = jnp.where(slot_col == dest_col, 1.0, 0.0).astype(BF16)

    n_chunks = len(chunks)
    crossing, sides, forwards = [], [], []

    def gather(c):
        off, lanes, row, rows = chunks[c]
        for copy in dispatches[c]:
            copy.wait_recv()
        x[t, :, off : off + lanes] = jnp.concatenate(
            [unpack(recv_d[e, row : row + rows], lanes, cap) for e in range(n_exp)], axis=0
        ).astype(BF16)
        part = x.at[t, :, pl.ds(off, lanes)]
        crossing.append(to_tensor(part, part, x_s.at[c], x_r.at[c], across))
        sides.append(to_tensor(part, part, sib_s.at[c], sib_r.at[c], sib))
        crossing[-1].start()
        sides[-1].start()

    def forward(c):
        off, lanes, _, _ = chunks[c]
        crossing[c].wait_recv()
        part = x.at[across, :, pl.ds(off, lanes)]
        forwards.append(to_tensor(part, part, fw_s.at[c], fw_r.at[c], sib))
        forwards[-1].start()

    tile = 512 if n_ff % 512 == 0 else 256

    def project(one, two, c, first, last):
        off, lanes, _, _ = chunks[c]
        feats = slice(off, off + lanes)
        rows_in = jnp.concatenate([x[one, :, feats], x[two, :, feats]], axis=1)
        for n in range(0, n_ff, tile):
            cols = slice(n, n + tile)

            def product(w):
                w_in = jnp.concatenate([w[one, feats, cols], w[two, feats, cols]], axis=0)
                return jnp.dot(rows_in, w_in, preferred_element_type=F32)

            gate, lift = product(wg), product(wu)
            if not first:
                gate = gate + acc_g[:, cols]
                lift = lift + acc_u[:, cols]
            if last:
                hidden[:, cols] = (jax.nn.silu(gate) * lift).astype(BF16)
            else:
                acc_g[:, cols] = gate
                acc_u[:, cols] = lift

    def near_pair(c):
        sides[c].wait_recv()
        project(t, sib, c, c == 0, False)

    def far_pair(c):
        forwards[c].wait_recv()
        project(across, diag, c, False, c == n_chunks - 1)

    gather(0)
    for c in range(1, n_chunks):
        gather(c)
        if c == 1:
            for load in gate_loads:
                load.wait()
        near_pair(c - 1)
        forward(c - 1)
        if c > 1:
            far_pair(c - 2)
    near_pair(n_chunks - 1)
    forward(n_chunks - 1)
    far_pair(n_chunks - 2)
    far_pair(n_chunks - 1)
    sends += crossing + sides + forwards
    for load in down_loads:
        load.wait()

    def partial(s, c):
        off, lanes, _, _ = chunks[c]
        return jnp.dot(hidden[...], wd[s, :, off : off + lanes], preferred_element_type=F32)

    back = list(range(n_chunks))[::-1]
    fars, halves, nears = {}, {}, {}

    def start_far(c):
        off, lanes, _, _ = chunks[c]
        far_out[:, off : off + lanes] = partial(diag, c)
        fars[c] = to_tensor(
            far_out.at[:, pl.ds(off, lanes)], far_in.at[:, pl.ds(off, lanes)], far_s.at[c], far_r.at[c], sib
        )
        fars[c].start()

    def start_half(c):
        off, lanes, _, _ = chunks[c]
        fars[c].wait_recv()
        half_out[:, off : off + lanes] = (
            far_own[:, off : off + lanes] + far_in[:, off : off + lanes]
        ).astype(BF16)
        halves[c] = to_tensor(
            half_out.at[:, pl.ds(off, lanes)], half_in.at[:, pl.ds(off, lanes)], half_s.at[c], half_r.at[c], across
        )
        halves[c].start()

    def start_near(c):
        off, lanes, _, _ = chunks[c]
        near_out[:, off : off + lanes] = partial(sib, c)
        nears[c] = to_tensor(
            near_out.at[:, pl.ds(off, lanes)], near_in.at[:, pl.ds(off, lanes)], near_s.at[c], near_r.at[c], sib
        )
        nears[c].start()

    start_far(back[0])
    for i, c in enumerate(back):
        off, lanes, _, _ = chunks[c]
        far_own[:, off : off + lanes] = partial(across, c)
        if i + 1 < n_chunks:
            start_far(back[i + 1])
        start_half(c)
    for c in back:
        start_near(c)
        off, lanes, _, _ = chunks[c]
        near_own[:, off : off + lanes] = partial(t, c)
    sends += list(fars.values()) + list(halves.values()) + list(nears.values())

    returns = {}
    for c in back:
        off, lanes, row, rows = chunks[c]
        nears[c].wait_recv()
        halves[c].wait_recv()
        total = (
            near_own[:, off : off + lanes] + near_in[:, off : off + lanes] + half_in[:, off : off + lanes].astype(F32)
        )
        for e in range(n_exp):
            send_r[e, row : row + rows] = pack(total[e * cap : (e + 1) * cap], lanes, rows).astype(BF16)
        copies = exchange(c, send_r, recv_r, rs_sem, rr_sem)
        for copy in copies:
            copy.start()
        recv_r[g, row : row + rows] = send_r[g, row : row + rows]
        returns[c] = copies
        sends += copies

    for c in back:
        off, lanes, row, rows = chunks[c]
        for copy in returns[c]:
            copy.wait_recv()
        returned = jnp.concatenate(
            [unpack(recv_r[e, row : row + rows], lanes, cap) for e in range(n_exp)], axis=0
        ).astype(BF16)
        out[:, off : off + lanes] = jnp.dot(combine[...], returned, preferred_element_type=F32).astype(BF16)

    for copy in sends:
        copy.wait_send()


def fused(tokens, route_logit, expert_ids, w_gate, w_up, w_down):
    n_exp = lax.axis_size("expert")
    n_ten = lax.axis_size("tensor")
    tok, width = tokens.shape
    n_ff = w_gate.shape[2]
    cap = 5 * tok // (4 * n_exp)
    slots = n_exp * cap
    chunks, block_rows = plan(width, cap)
    n_c = len(chunks)
    dma = pltpu.SemaphoreType.DMA
    vmem = pltpu.VMEM
    blocks = (n_exp, block_rows, 128)
    return pl.pallas_call(
        functools.partial(kernel, n_exp, n_ten, cap, chunks),
        out_shape=jax.ShapeDtypeStruct((tok, width), BF16),
        in_specs=[pl.BlockSpec(memory_space=pl.ANY)] * 6,
        out_specs=pl.BlockSpec(memory_space=vmem),
        scratch_shapes=[
            vmem((tok, width), BF16),
            vmem((1, tok), F32),
            vmem((1, tok), jnp.int32),
            vmem((n_ten, width, n_ff), BF16),
            vmem((n_ten, width, n_ff), BF16),
            vmem((n_ten, n_ff, width), BF16),
            vmem(blocks, BF16),
            vmem(blocks, BF16),
            vmem(blocks, BF16),
            vmem(blocks, BF16),
            vmem((n_ten, slots, width), BF16),
            vmem((slots, n_ff), F32),
            vmem((slots, n_ff), F32),
            vmem((slots, n_ff), BF16),
            vmem((tok, slots), BF16),
            vmem((slots, width), F32),
            vmem((slots, width), F32),
            vmem((slots, width), F32),
            vmem((slots, width), F32),
            vmem((slots, width), F32),
            vmem((slots, width), F32),
            vmem((slots, width), BF16),
            vmem((slots, width), BF16),
            dma((3,)),
            dma((3, n_ten)),
        ]
        + [dma((n_exp, n_c))] * 4
        + [dma((n_c,))] * 12,
        compiler_params=pltpu.CompilerParams(
            collective_id=0, has_side_effects=True, vmem_limit_bytes=LIMIT
        ),
        cost_estimate=pl.CostEstimate(
            flops=6 * slots * n_ten * width * n_ff,
            bytes_accessed=6 * n_ten * width * n_ff,
            transcendentals=slots * n_ff,
        ),
    )(tokens, route_logit.reshape(1, tok), expert_ids.reshape(1, tok), w_gate, w_up, w_down)


def on_device(tokens, route_logit, expert_ids, w_gate, w_up, w_down):
    expert_count = lax.axis_size("expert")
    tok_rows, width_local = tokens.shape
    capacity = 5 * tok_rows // (4 * expert_count)
    if (
        lax.axis_size("tensor") == 4
        and capacity % 8 == 0
        and width_local % 128 == 0
        and w_gate.shape[2] % 256 == 0
        and expert_count <= 8
    ):
        return fused(tokens, route_logit, expert_ids, w_gate, w_up, w_down)
    slot_count = expert_count * capacity
    route = expert_ids[:, 0]
    one_hot = (route[:, None] == jnp.arange(expert_count, dtype=jnp.int32)[None, :]).astype(
        jnp.int32
    )
    earlier = jnp.cumsum(one_hot, axis=0) - one_hot
    position = jnp.sum(earlier * one_hot, axis=1)
    destination = route * capacity + position
    dispatch_map = (
        jnp.arange(slot_count, dtype=jnp.int32)[:, None] == destination[None, :]
    ).astype(jnp.bfloat16)
    factor = jax.nn.sigmoid(route_logit)
    scaled = (factor[:, None] * tokens.astype(jnp.float32)).astype(jnp.bfloat16)
    outgoing = jnp.dot(dispatch_map, scaled, preferred_element_type=jnp.float32).astype(
        jnp.bfloat16
    )
    outgoing = outgoing.reshape(expert_count, capacity, width_local)
    arrived = lax.all_to_all(outgoing, "expert", split_axis=0, concat_axis=0, tiled=True).reshape(
        slot_count, width_local
    )
    gate_local = w_gate[0]
    lift_local = w_up[0]
    down_local = w_down[0]
    piece = lax.all_gather(arrived, "tensor", axis=1, tiled=True)
    gate_val = jnp.dot(piece, gate_local, preferred_element_type=jnp.float32)
    lift_val = jnp.dot(piece, lift_local, preferred_element_type=jnp.float32)
    hidden = (jax.nn.silu(gate_val) * lift_val).astype(jnp.bfloat16)
    summed = lax.psum_scatter(
        lax.dot_general(
            down_local, hidden, (((0,), (1,)), ((), ())), preferred_element_type=jnp.float32
        ),
        "tensor",
        scatter_dimension=0,
        tiled=True,
    )
    expert_out = summed.astype(jnp.bfloat16).reshape(width_local, expert_count, capacity)
    returned = lax.all_to_all(
        expert_out, "expert", split_axis=1, concat_axis=1, tiled=True
    ).reshape(width_local, slot_count)
    mixed = lax.dot_general(
        dispatch_map, returned, (((0,), (1,)), ((), ())), preferred_element_type=jnp.float32
    )
    return mixed.astype(jnp.bfloat16)


def solution(mesh):
    return jax.shard_map(
        on_device,
        mesh=mesh,
        in_specs=(
            P("expert", "tensor"),
            P("expert"),
            P("expert", None),
            P("expert", None, "tensor"),
            P("expert", None, "tensor"),
            P("expert", "tensor", None),
        ),
        out_specs=P("expert", "tensor"),
        check_vma=False,
    )
```

```python
import functools

import jax
import jax.numpy as jnp
from jax import lax
from jax.experimental import pallas as pl
from jax.experimental.pallas import tpu as pltpu
from jax.sharding import PartitionSpec as P

MESH = pl.DeviceIdType.MESH
LIMIT = 63 * 1024 * 1024
F32 = jnp.float32
BF16 = jnp.bfloat16


def plan(width, cap):
    chunks, off, row = [], 0, 0
    while off < width:
        lanes = min(256, width - off)
        rows = -(-(cap * (lanes // 128)) // 16) * 16
        chunks.append((off, lanes, row, rows))
        off, row = off + lanes, row + rows
    return chunks, row


def pack(block, lanes, rows):
    parts = [block[:, i : i + 128] for i in range(0, lanes, 128)]
    spare = rows - block.shape[0] * len(parts)
    if spare:
        parts.append(jnp.zeros((spare, 128), F32))
    return jnp.concatenate(parts, axis=0) if len(parts) > 1 else parts[0]


def unpack(packed, lanes, cap):
    packed = packed.astype(F32)
    parts = [packed[i * cap : (i + 1) * cap] for i in range(lanes // 128)]
    return jnp.concatenate(parts, axis=1) if len(parts) > 1 else parts[0]


def cut(cap):
    first = 24 if cap == 40 else cap
    return [(0, first)] + ([(first, cap - first)] if cap > first else [])


def kernel(n_exp, n_ten, cap, batches, plans, names, *refs):
    r = dict(zip(names, refs))
    tokens, logit, ids = r["tokens"], r["logit"], r["ids"]
    wg, wu, wd, combine, out = r["wg"], r["wu"], r["wd"], r["combine"], r["out"]
    w_sem = r["w_sem"]
    g = lax.axis_index("expert")
    t = lax.axis_index("tensor")
    sib = t + 1 - 2 * lax.rem(t, 2)
    across = lax.rem(t + 2, 4)
    diag = lax.rem(sib + 2, 4)
    tok, width = tokens.shape
    n_ff = wg.shape[2]
    n_chunks = len(plans[0])
    tile = 512 if n_ff % 512 == 0 else 256
    order = list(range(1, n_exp))
    all_b = range(len(batches))

    small = [
        pltpu.make_async_copy(r[name + "_in"], r[name], r["in_sem"].at[i])
        for i, name in enumerate(("ids", "logit", "tokens"))
    ]
    for copy in small:
        copy.start()

    barrier = pltpu.get_barrier_semaphore()
    for k in order:
        pl.semaphore_signal(barrier, inc=1, device_id=(lax.rem(g + k, n_exp), t), device_id_type=MESH)
    for peer in (sib, across):
        pl.semaphore_signal(barrier, inc=1, device_id=(g, peer), device_id_type=MESH)

    small[0].wait()
    ids_row = ids[...]
    one_hot = lax.broadcasted_iota(jnp.int32, (n_exp, tok), 0) == ids_row
    older = lax.broadcasted_iota(jnp.int32, (tok, tok), 0)
    newer = lax.broadcasted_iota(jnp.int32, (tok, tok), 1)
    before = jnp.where(older < newer, 1.0, 0.0).astype(BF16)
    hot = jnp.where(one_hot, 1.0, 0.0)
    earlier = jnp.dot(hot.astype(BF16), before, preferred_element_type=F32)
    position = jnp.sum(earlier * hot, axis=0, keepdims=True)
    dest = ids_row.astype(F32) * float(cap) + position
    eye = older == newer
    dispatch = []
    for first, rows in batches:
        row = lax.broadcasted_iota(jnp.int32, (rows, tok), 0)
        slot = jnp.concatenate([row + (e * cap + first) for e in range(n_exp)], axis=0).astype(F32)
        dispatch.append(jnp.where(slot == dest, 1.0, 0.0).astype(BF16))
    small[1].wait()
    factor = jnp.sum(jnp.where(eye, jax.nn.sigmoid(logit[...]), 0.0), axis=1, keepdims=True)

    def exchange(b, c, kind):
        _, _, row, rows = plans[b][c]
        src, dst = r["send_" + kind][b], r["recv_" + kind][b]
        copies = []
        for k in order:
            e = lax.rem(g + k, n_exp)
            copies.append(
                pltpu.make_async_remote_copy(
                    src_ref=src.at[e, pl.ds(row, rows)],
                    dst_ref=dst.at[g, pl.ds(row, rows)],
                    send_sem=r["s_" + kind].at[b, k, c],
                    recv_sem=r["r_" + kind].at[b, k, c],
                    device_id=(e, t),
                    device_id_type=MESH,
                )
            )
        return copies

    def to_tensor(src, dst, kind, b, c, peer):
        return pltpu.make_async_remote_copy(
            src_ref=src,
            dst_ref=dst,
            send_sem=r["s_" + kind].at[b, c],
            recv_sem=r["r_" + kind].at[b, c],
            device_id=(g, peer),
            device_id_type=MESH,
        )

    def post(b, c, kind, values):
        _, lanes, row, rows = plans[b][c]
        n = batches[b][1]
        src, dst = r["send_" + kind][b], r["recv_" + kind][b]
        for e in range(n_exp):
            src[e, row : row + rows] = pack(values[e * n : (e + 1) * n], lanes, rows).astype(BF16)
        copies = exchange(b, c, kind)
        if kind == "d" and b == 0 and c == 0:
            pl.semaphore_wait(barrier, n_exp - 1 + 2)
        for copy in copies:
            copy.start()
        dst[g, row : row + rows] = src[g, row : row + rows]
        sends.extend(copies)
        return copies

    def collect(b, c, kind, copies):
        _, lanes, row, rows = plans[b][c]
        for copy in copies:
            copy.wait_recv()
        src = r["recv_" + kind][b]
        return jnp.concatenate(
            [unpack(src[e, row : row + rows], lanes, batches[b][1]) for e in range(n_exp)], axis=0
        ).astype(BF16)

    sends = []
    small[2].wait()
    scaled = (factor * tokens[...].astype(F32)).astype(BF16)
    dispatches = {}
    for b in all_b:
        for c in range(n_chunks):
            off, lanes, _, _ = plans[b][c]
            outgoing = jnp.dot(dispatch[b], scaled[:, off : off + lanes], preferred_element_type=F32)
            dispatches[b, c] = post(b, c, "d", outgoing)

    w_loads, down_loads = [], []
    for i, s in enumerate((t, sib, across, diag)):
        rows_of = pl.ds(pl.multiple_of(s * width, 128), width)
        w_loads.append(pltpu.make_async_copy(r["w_gate"].at[0, rows_of], wg.at[s], w_sem.at[0, i]))
        w_loads.append(pltpu.make_async_copy(r["w_up"].at[0, rows_of], wu.at[s], w_sem.at[1, i]))
    for s in range(n_ten):
        down_loads.append(
            pltpu.make_async_copy(r["w_down"].at[0, :, pl.ds(s * width, width)], wd.at[s], w_sem.at[2, s])
        )
    for load in w_loads + down_loads:
        load.start()

    dest_col = jnp.sum(jnp.where(eye, dest, 0.0), axis=1, keepdims=True)
    for b, (first, rows) in enumerate(batches):
        lane = lax.broadcasted_iota(jnp.int32, (1, n_exp * rows), 1)
        slot = lane + first
        for e in range(1, n_exp):
            slot = slot + jnp.where(lane >= e * rows, cap - rows, 0)
        combine[b][...] = jnp.where(slot.astype(F32) == dest_col, 1.0, 0.0).astype(BF16)

    crossing, sides, forwards = {}, {}, {}

    def gather(b, c):
        off, lanes, _, _ = plans[b][c]
        x = r["x"][b]
        x[t, :, off : off + lanes] = collect(b, c, "d", dispatches[b, c])
        part = x.at[t, :, pl.ds(off, lanes)]
        crossing[b, c] = to_tensor(part, part, "cross", b, c, across)
        sides[b, c] = to_tensor(part, part, "side", b, c, sib)
        crossing[b, c].start()
        sides[b, c].start()

    def forward(b, c):
        off, lanes, _, _ = plans[b][c]
        crossing[b, c].wait_recv()
        part = r["x"][b].at[across, :, pl.ds(off, lanes)]
        forwards[b, c] = to_tensor(part, part, "fwd", b, c, sib)
        forwards[b, c].start()

    def project(b, c, one, two, begin, end):
        off, lanes, _, _ = plans[b][c]
        x, acc_g, acc_u, hidden = r["x"][b], r["acc_g"][b], r["acc_u"][b], r["hidden"][b]
        feats = slice(off, off + lanes)
        rows_in = jnp.concatenate([x[one, :, feats], x[two, :, feats]], axis=1)
        for n in range(0, n_ff, tile):
            cols = slice(n, n + tile)

            def product(w):
                w_in = jnp.concatenate([w[one, feats, cols], w[two, feats, cols]], axis=0)
                return jnp.dot(rows_in, w_in, preferred_element_type=F32)

            gate, lift = product(wg), product(wu)
            if not begin:
                gate = gate + acc_g[:, cols]
                lift = lift + acc_u[:, cols]
            if end:
                hidden[:, cols] = (jax.nn.silu(gate) * lift).astype(BF16)
            else:
                acc_g[:, cols] = gate
                acc_u[:, cols] = lift

    def near_pair(b, c):
        sides[b, c].wait_recv()
        project(b, c, t, sib, c == 0, False)

    def far_pair(b, c):
        forwards[b, c].wait_recv()
        project(b, c, across, diag, False, c == n_chunks - 1)

    back = list(range(n_chunks))[::-1]
    fars, halves, nears, returns = {}, {}, {}, {}

    def partial(b, s, c):
        off, lanes, _, _ = plans[b][c]
        return jnp.dot(r["hidden"][b][...], wd[s, :, off : off + lanes], preferred_element_type=F32)

    def start_far(b, c):
        off, lanes, _, _ = plans[b][c]
        part = pl.ds(off, lanes)
        r["far_out"][b][:, off : off + lanes] = partial(b, diag, c)
        fars[b, c] = to_tensor(r["far_out"][b].at[:, part], r["far_in"][b].at[:, part], "far", b, c, sib)
        fars[b, c].start()

    def start_half(b, c):
        off, lanes, _, _ = plans[b][c]
        part, lane = pl.ds(off, lanes), slice(off, off + lanes)
        fars[b, c].wait_recv()
        r["half_out"][b][:, lane] = (r["far_own"][b][:, lane] + r["far_in"][b][:, lane]).astype(BF16)
        halves[b, c] = to_tensor(r["half_out"][b].at[:, part], r["half_in"][b].at[:, part], "half", b, c, across)
        halves[b, c].start()

    def far_side(b):
        start_far(b, back[0])
        for i, c in enumerate(back):
            off, lanes, _, _ = plans[b][c]
            r["far_own"][b][:, off : off + lanes] = partial(b, across, c)
            if i + 1 < n_chunks:
                start_far(b, back[i + 1])
            start_half(b, c)

    def near_side(b):
        for c in back:
            off, lanes, _, _ = plans[b][c]
            part = pl.ds(off, lanes)
            r["near_out"][b][:, off : off + lanes] = partial(b, sib, c)
            nears[b, c] = to_tensor(r["near_out"][b].at[:, part], r["near_in"][b].at[:, part], "near", b, c, sib)
            nears[b, c].start()
            r["near_own"][b][:, off : off + lanes] = partial(b, t, c)

    def give_back(b, c):
        off, lanes, _, _ = plans[b][c]
        lane = slice(off, off + lanes)
        nears[b, c].wait_recv()
        halves[b, c].wait_recv()
        total = (
            r["near_own"][b][:, lane] + r["near_in"][b][:, lane] + r["half_in"][b][:, lane].astype(F32)
        )
        returns[b, c] = post(b, c, "r", total)

    last = n_chunks - 1

    def first_batch(b):
        gather(b, 0)
        for c in range(1, n_chunks):
            gather(b, c)
            if c == 1:
                for load in w_loads[:4]:
                    load.wait()
            near_pair(b, c - 1)
            forward(b, c - 1)
            if c > 1:
                if c == 2:
                    for load in w_loads[4:]:
                        load.wait()
                far_pair(b, c - 2)
        near_pair(b, last)

    first_batch(0)
    if len(batches) == 1:
        forward(0, last)
        far_pair(0, last - 1)
        far_pair(0, last)
        for load in down_loads:
            load.wait()
        far_side(0)
        near_side(0)
        for c in back:
            give_back(0, c)
    else:
        gather(1, 0)
        forward(0, last)
        far_pair(0, last - 1)
        for c in range(1, n_chunks):
            gather(1, c)
        far_pair(0, last)
        for load in down_loads:
            load.wait()
        forward(1, 0)
        far_side(0)
        for c in range(1, n_chunks):
            forward(1, c)
        near_side(0)
        for c in range(n_chunks):
            near_pair(1, c)
        for c in range(n_chunks):
            give_back(0, back[c])
            far_pair(1, c)
        far_side(1)
        near_side(1)
        for c in back:
            give_back(1, c)

    for c in back:
        off, lanes, _, _ = plans[0][c]
        mixed = None
        for b in all_b:
            term = jnp.dot(combine[b][...], collect(b, c, "r", returns[b, c]), preferred_element_type=F32)
            mixed = term if mixed is None else mixed + term
        out[:, off : off + lanes] = mixed.astype(BF16)

    for group in (crossing, sides, forwards, fars, halves, nears):
        sends.extend(group.values())
    for copy in sends:
        copy.wait_send()


def grouped(n_b, single, per_batch, n_exp, n_ten, cap, batches, plans, *refs):
    refs = list(refs)
    names, values = [], []
    for name in single:
        names.append(name)
        values.append(refs.pop(0))
    for name in per_batch:
        names.append(name)
        values.append([refs.pop(0) for _ in range(n_b)])
    kernel(n_exp, n_ten, cap, batches, plans, names, *values)


def fused(tokens, route_logit, expert_ids, w_gate, w_up, w_down):
    n_exp = lax.axis_size("expert")
    n_ten = lax.axis_size("tensor")
    tok, width = tokens.shape
    n_ff = w_gate.shape[2]
    cap = 5 * tok // (4 * n_exp)
    slots = n_exp * cap
    batches = cut(cap)
    made = [plan(width, rows) for _, rows in batches]
    plans = [chunks for chunks, _ in made]
    n_b, n_c = len(batches), len(plans[0])
    vmem, dma = pltpu.VMEM, pltpu.SemaphoreType.DMA
    scratch = {
        "tokens": vmem((tok, width), BF16),
        "logit": vmem((1, tok), F32),
        "ids": vmem((1, tok), jnp.int32),
        "wg": vmem((n_ten, width, n_ff), BF16),
        "wu": vmem((n_ten, width, n_ff), BF16),
        "wd": vmem((n_ten, n_ff, width), BF16),
        "in_sem": dma((3,)),
        "w_sem": dma((3, n_ten)),
    }
    for kind in ("d", "r"):
        scratch["s_" + kind] = dma((n_b, n_exp, n_c))
        scratch["r_" + kind] = dma((n_b, n_exp, n_c))
    for kind in ("cross", "side", "fwd", "far", "half", "near"):
        scratch["s_" + kind] = dma((n_b, n_c))
        scratch["r_" + kind] = dma((n_b, n_c))
    lists = {}
    for name in ("send_d", "recv_d", "send_r", "recv_r"):
        lists[name] = [vmem((n_exp, block, 128), BF16) for _, block in made]
    counts = [n_exp * rows for _, rows in batches]
    lists["x"] = [vmem((n_ten, n, width), BF16) for n in counts]
    for name in ("acc_g", "acc_u"):
        lists[name] = [vmem((n, n_ff), F32) for n in counts]
    lists["hidden"] = [vmem((n, n_ff), BF16) for n in counts]
    lists["combine"] = [vmem((tok, n), BF16) for n in counts]
    for name in ("far_out", "far_in", "far_own", "near_out", "near_in", "near_own"):
        lists[name] = [vmem((n, width), F32) for n in counts]
    for name in ("half_out", "half_in"):
        lists[name] = [vmem((n, width), BF16) for n in counts]
    single = ["tokens_in", "logit_in", "ids_in", "w_gate", "w_up", "w_down", "out"] + list(scratch)
    return pl.pallas_call(
        functools.partial(grouped, n_b, single, list(lists), n_exp, n_ten, cap, batches, plans),
        out_shape=jax.ShapeDtypeStruct((tok, width), BF16),
        in_specs=[pl.BlockSpec(memory_space=pl.ANY)] * 6,
        out_specs=pl.BlockSpec(memory_space=vmem),
        scratch_shapes=list(scratch.values()) + [ref for group in lists.values() for ref in group],
        compiler_params=pltpu.CompilerParams(
            collective_id=0, has_side_effects=True, vmem_limit_bytes=LIMIT
        ),
        cost_estimate=pl.CostEstimate(
            flops=6 * slots * n_ten * width * n_ff,
            bytes_accessed=6 * n_ten * width * n_ff,
            transcendentals=slots * n_ff,
        ),
    )(tokens, route_logit.reshape(1, tok), expert_ids.reshape(1, tok), w_gate, w_up, w_down)


def on_device(tokens, route_logit, expert_ids, w_gate, w_up, w_down):
    expert_count = lax.axis_size("expert")
    tok_rows, width_local = tokens.shape
    capacity = 5 * tok_rows // (4 * expert_count)
    if (
        lax.axis_size("tensor") == 4
        and capacity % 8 == 0
        and width_local % 128 == 0
        and w_gate.shape[2] % 256 == 0
        and expert_count <= 8
    ):
        return fused(tokens, route_logit, expert_ids, w_gate, w_up, w_down)
    slot_count = expert_count * capacity
    route = expert_ids[:, 0]
    one_hot = (route[:, None] == jnp.arange(expert_count, dtype=jnp.int32)[None, :]).astype(
        jnp.int32
    )
    earlier = jnp.cumsum(one_hot, axis=0) - one_hot
    position = jnp.sum(earlier * one_hot, axis=1)
    destination = route * capacity + position
    dispatch_map = (
        jnp.arange(slot_count, dtype=jnp.int32)[:, None] == destination[None, :]
    ).astype(jnp.bfloat16)
    factor = jax.nn.sigmoid(route_logit)
    scaled = (factor[:, None] * tokens.astype(jnp.float32)).astype(jnp.bfloat16)
    outgoing = jnp.dot(dispatch_map, scaled, preferred_element_type=jnp.float32).astype(
        jnp.bfloat16
    )
    outgoing = outgoing.reshape(expert_count, capacity, width_local)
    arrived = lax.all_to_all(outgoing, "expert", split_axis=0, concat_axis=0, tiled=True).reshape(
        slot_count, width_local
    )
    gate_local = w_gate[0]
    lift_local = w_up[0]
    down_local = w_down[0]
    piece = lax.all_gather(arrived, "tensor", axis=1, tiled=True)
    gate_val = jnp.dot(piece, gate_local, preferred_element_type=jnp.float32)
    lift_val = jnp.dot(piece, lift_local, preferred_element_type=jnp.float32)
    hidden = (jax.nn.silu(gate_val) * lift_val).astype(jnp.bfloat16)
    summed = lax.psum_scatter(
        lax.dot_general(
            down_local, hidden, (((0,), (1,)), ((), ())), preferred_element_type=jnp.float32
        ),
        "tensor",
        scatter_dimension=0,
        tiled=True,
    )
    expert_out = summed.astype(jnp.bfloat16).reshape(width_local, expert_count, capacity)
    returned = lax.all_to_all(
        expert_out, "expert", split_axis=1, concat_axis=1, tiled=True
    ).reshape(width_local, slot_count)
    mixed = lax.dot_general(
        dispatch_map, returned, (((0,), (1,)), ((), ())), preferred_element_type=jnp.float32
    )
    return mixed.astype(jnp.bfloat16)


def solution(mesh):
    return jax.shard_map(
        on_device,
        mesh=mesh,
        in_specs=(
            P("expert", "tensor"),
            P("expert"),
            P("expert", None),
            P("expert", None, "tensor"),
            P("expert", None, "tensor"),
            P("expert", "tensor", None),
        ),
        out_specs=P("expert", "tensor"),
        check_vma=False,
    )
```

```python
import functools

import jax
import jax.numpy as jnp
from jax import lax
from jax.experimental import pallas as pl
from jax.experimental.pallas import tpu as pltpu
from jax.sharding import PartitionSpec as P

MESH = pl.DeviceIdType.MESH
LIMIT = 63 * 1024 * 1024
F32 = jnp.float32
BF16 = jnp.bfloat16


def plan(width, cap):
    chunks, off, row = [], 0, 0
    while off < width:
        lanes = min(256, width - off)
        rows = -(-(cap * (lanes // 128)) // 16) * 16
        chunks.append((off, lanes, row, rows))
        off, row = off + lanes, row + rows
    return chunks, row


def pack(block, lanes, rows):
    parts = [block[:, i : i + 128] for i in range(0, lanes, 128)]
    spare = rows - block.shape[0] * len(parts)
    if spare:
        parts.append(jnp.zeros((spare, 128), F32))
    return jnp.concatenate(parts, axis=0) if len(parts) > 1 else parts[0]


def unpack(packed, lanes, cap):
    packed = packed.astype(F32)
    parts = [packed[i * cap : (i + 1) * cap] for i in range(lanes // 128)]
    return jnp.concatenate(parts, axis=1) if len(parts) > 1 else parts[0]


def cut(cap):
    return [(0, cap)]


def kernel(n_exp, n_ten, cap, batches, plans, names, *refs):
    r = dict(zip(names, refs))
    tokens, logit, ids = r["tokens"], r["logit"], r["ids"]
    wg, wu, wd, combine, out = r["wg"], r["wu"], r["wd"], r["combine"], r["out"]
    w_sem = r["w_sem"]
    g = lax.axis_index("expert")
    t = lax.axis_index("tensor")
    sib = t + 1 - 2 * lax.rem(t, 2)
    across = lax.rem(t + 2, 4)
    diag = lax.rem(sib + 2, 4)
    tok, width = tokens.shape
    n_ff = wg.shape[2]
    n_chunks = len(plans[0])
    tile = 512 if n_ff % 512 == 0 else 256
    order = list(range(1, n_exp))
    all_b = range(len(batches))

    small = [
        pltpu.make_async_copy(r[name + "_in"], r[name], r["in_sem"].at[i])
        for i, name in enumerate(("ids", "logit", "tokens"))
    ]
    for copy in small:
        copy.start()

    barrier = pltpu.get_barrier_semaphore()
    for k in order:
        pl.semaphore_signal(barrier, inc=1, device_id=(lax.rem(g + k, n_exp), t), device_id_type=MESH)
    for peer in (sib, across):
        pl.semaphore_signal(barrier, inc=1, device_id=(g, peer), device_id_type=MESH)

    w_loads, down_loads = [], []
    for i, s in enumerate((t, sib, across, diag)):
        rows_of = pl.ds(pl.multiple_of(s * width, 128), width)
        w_loads.append(pltpu.make_async_copy(r["w_gate"].at[0, rows_of], wg.at[s], w_sem.at[0, i]))
        w_loads.append(pltpu.make_async_copy(r["w_up"].at[0, rows_of], wu.at[s], w_sem.at[1, i]))
    for s in range(n_ten):
        down_loads.append(
            pltpu.make_async_copy(r["w_down"].at[0, :, pl.ds(s * width, width)], wd.at[s], w_sem.at[2, s])
        )

    small[0].wait()
    ids_row = ids[...]
    one_hot = lax.broadcasted_iota(jnp.int32, (n_exp, tok), 0) == ids_row
    older = lax.broadcasted_iota(jnp.int32, (tok, tok), 0)
    newer = lax.broadcasted_iota(jnp.int32, (tok, tok), 1)
    before = jnp.where(older < newer, 1.0, 0.0).astype(BF16)
    hot = jnp.where(one_hot, 1.0, 0.0)
    earlier = jnp.dot(hot.astype(BF16), before, preferred_element_type=F32)
    position = jnp.sum(earlier * hot, axis=0, keepdims=True)
    dest = ids_row.astype(F32) * float(cap) + position
    eye = older == newer
    dispatch = []
    for first, rows in batches:
        row = lax.broadcasted_iota(jnp.int32, (rows, tok), 0)
        slot = jnp.concatenate([row + (e * cap + first) for e in range(n_exp)], axis=0).astype(F32)
        dispatch.append(jnp.where(slot == dest, 1.0, 0.0).astype(BF16))
    small[1].wait()
    factor = jnp.sum(jnp.where(eye, jax.nn.sigmoid(logit[...]), 0.0), axis=1, keepdims=True)

    def exchange(b, c, kind):
        _, _, row, rows = plans[b][c]
        src, dst = r["send_" + kind][b], r["recv_" + kind][b]
        copies = []
        for k in order:
            e = lax.rem(g + k, n_exp)
            copies.append(
                pltpu.make_async_remote_copy(
                    src_ref=src.at[e, pl.ds(row, rows)],
                    dst_ref=dst.at[g, pl.ds(row, rows)],
                    send_sem=r["s_" + kind].at[b, k, c],
                    recv_sem=r["r_" + kind].at[b, k, c],
                    device_id=(e, t),
                    device_id_type=MESH,
                )
            )
        return copies

    def to_tensor(src, dst, kind, b, c, peer):
        return pltpu.make_async_remote_copy(
            src_ref=src,
            dst_ref=dst,
            send_sem=r["s_" + kind].at[b, c],
            recv_sem=r["r_" + kind].at[b, c],
            device_id=(g, peer),
            device_id_type=MESH,
        )

    def post(b, c, kind, values):
        _, lanes, row, rows = plans[b][c]
        n = batches[b][1]
        src, dst = r["send_" + kind][b], r["recv_" + kind][b]
        for e in range(n_exp):
            src[e, row : row + rows] = pack(values[e * n : (e + 1) * n], lanes, rows).astype(BF16)
        copies = exchange(b, c, kind)
        if kind == "d" and b == 0 and c == 0:
            pl.semaphore_wait(barrier, n_exp - 1 + 2)
        for copy in copies:
            copy.start()
        dst[g, row : row + rows] = src[g, row : row + rows]
        sends.extend(copies)
        return copies

    def collect(b, c, kind, copies):
        _, lanes, row, rows = plans[b][c]
        for copy in copies:
            copy.wait_recv()
        src = r["recv_" + kind][b]
        return jnp.concatenate(
            [unpack(src[e, row : row + rows], lanes, batches[b][1]) for e in range(n_exp)], axis=0
        ).astype(BF16)

    sends = []
    small[2].wait()
    for load in w_loads[:4]:
        load.start()
    scaled = (factor * tokens[...].astype(F32)).astype(BF16)
    dispatches = {}
    for b in all_b:
        for c in range(n_chunks):
            off, lanes, _, _ = plans[b][c]
            outgoing = jnp.dot(dispatch[b], scaled[:, off : off + lanes], preferred_element_type=F32)
            dispatches[b, c] = post(b, c, "d", outgoing)

    for load in w_loads[4:] + down_loads:
        load.start()

    dest_col = jnp.sum(jnp.where(eye, dest, 0.0), axis=1, keepdims=True)
    for b, (first, rows) in enumerate(batches):
        lane = lax.broadcasted_iota(jnp.int32, (1, n_exp * rows), 1)
        slot = lane + first
        for e in range(1, n_exp):
            slot = slot + jnp.where(lane >= e * rows, cap - rows, 0)
        combine[b][...] = jnp.where(slot.astype(F32) == dest_col, 1.0, 0.0).astype(BF16)

    crossing, sides, forwards = {}, {}, {}

    def gather(b, c):
        off, lanes, _, _ = plans[b][c]
        x = r["x"][b]
        x[t, :, off : off + lanes] = collect(b, c, "d", dispatches[b, c])
        part = x.at[t, :, pl.ds(off, lanes)]
        crossing[b, c] = to_tensor(part, part, "cross", b, c, across)
        sides[b, c] = to_tensor(part, part, "side", b, c, sib)
        crossing[b, c].start()
        sides[b, c].start()

    def forward(b, c):
        off, lanes, _, _ = plans[b][c]
        crossing[b, c].wait_recv()
        part = r["x"][b].at[across, :, pl.ds(off, lanes)]
        forwards[b, c] = to_tensor(part, part, "fwd", b, c, sib)
        forwards[b, c].start()

    def project(b, c, one, two, begin, end):
        off, lanes, _, _ = plans[b][c]
        x, acc_g, acc_u, hidden = r["x"][b], r["acc_g"][b], r["acc_u"][b], r["hidden"][b]
        feats = slice(off, off + lanes)
        rows_in = jnp.concatenate([x[one, :, feats], x[two, :, feats]], axis=1)
        for n in range(0, n_ff, tile):
            cols = slice(n, n + tile)

            def product(w):
                w_in = jnp.concatenate([w[one, feats, cols], w[two, feats, cols]], axis=0)
                return jnp.dot(rows_in, w_in, preferred_element_type=F32)

            gate, lift = product(wg), product(wu)
            if not begin:
                gate = gate + acc_g[:, cols]
                lift = lift + acc_u[:, cols]
            if end:
                hidden[:, cols] = ((0.5 * gate) * (1.0 + jnp.tanh(0.5 * gate)) * lift).astype(BF16)
            else:
                acc_g[:, cols] = gate
                acc_u[:, cols] = lift

    def near_pair(b, c):
        sides[b, c].wait_recv()
        project(b, c, t, sib, c == 0, False)

    def far_pair(b, c):
        forwards[b, c].wait_recv()
        project(b, c, across, diag, False, c == n_chunks - 1)

    back = list(range(n_chunks))[::-1]
    fars, halves, nears, returns = {}, {}, {}, {}

    def partials(b, one, two, c):
        off, lanes, _, _ = plans[b][c]
        rows_in, part = r["hidden"][b][...], slice(off, off + lanes)
        if lanes == 128:
            both = jnp.dot(
                rows_in,
                jnp.concatenate([wd[one, :, part], wd[two, :, part]], axis=1),
                preferred_element_type=F32,
            )
            return (lambda: both[:, :lanes]), (lambda: both[:, lanes:])
        return tuple(
            functools.partial(jnp.dot, rows_in, wd[s, :, part], preferred_element_type=F32) for s in (one, two)
        )

    def start_far(b, c):
        off, lanes, _, _ = plans[b][c]
        part = pl.ds(off, lanes)
        theirs, mine = partials(b, diag, across, c)
        r["far_out"][b][:, off : off + lanes] = theirs()
        fars[b, c] = to_tensor(r["far_out"][b].at[:, part], r["far_in"][b].at[:, part], "far", b, c, sib)
        fars[b, c].start()
        r["far_own"][b][:, off : off + lanes] = mine()

    def start_half(b, c):
        off, lanes, _, _ = plans[b][c]
        part, lane = pl.ds(off, lanes), slice(off, off + lanes)
        fars[b, c].wait_recv()
        r["half_out"][b][:, lane] = (r["far_own"][b][:, lane] + r["far_in"][b][:, lane]).astype(BF16)
        halves[b, c] = to_tensor(r["half_out"][b].at[:, part], r["half_in"][b].at[:, part], "half", b, c, across)
        halves[b, c].start()

    def far_side(b):
        start_far(b, back[0])
        for i, c in enumerate(back):
            if i + 1 < n_chunks:
                start_far(b, back[i + 1])
            start_half(b, c)

    def near_side(b):
        for c in back:
            off, lanes, _, _ = plans[b][c]
            part = pl.ds(off, lanes)
            theirs, mine = partials(b, sib, t, c)
            r["near_out"][b][:, off : off + lanes] = theirs()
            nears[b, c] = to_tensor(r["near_out"][b].at[:, part], r["near_in"][b].at[:, part], "near", b, c, sib)
            nears[b, c].start()
            r["near_own"][b][:, off : off + lanes] = mine()

    def give_back(b, c):
        off, lanes, _, _ = plans[b][c]
        lane = slice(off, off + lanes)
        nears[b, c].wait_recv()
        halves[b, c].wait_recv()
        total = (
            r["near_own"][b][:, lane] + r["near_in"][b][:, lane] + r["half_in"][b][:, lane].astype(F32)
        )
        returns[b, c] = post(b, c, "r", total)

    last = n_chunks - 1

    gather(0, 0)
    for load in w_loads[:4]:
        load.wait()
    near_pair(0, 0)
    for c in range(1, n_chunks):
        gather(0, c)
        if c == 1:
            forward(0, 0)
        if c < last:
            near_pair(0, c)
    for load in w_loads[4:]:
        load.wait()
    far_pair(0, 0)
    for c in range(1, last):
        forward(0, c)
    near_pair(0, last)
    forward(0, last)
    for c in range(1, n_chunks):
        far_pair(0, c)
    for load in down_loads:
        load.wait()
    far_side(0)
    near_side(0)
    for c in back:
        give_back(0, c)

    for c in back:
        off, lanes, _, _ = plans[0][c]
        mixed = None
        for b in all_b:
            term = jnp.dot(combine[b][...], collect(b, c, "r", returns[b, c]), preferred_element_type=F32)
            mixed = term if mixed is None else mixed + term
        out[:, off : off + lanes] = mixed.astype(BF16)

    for group in (crossing, sides, forwards, fars, halves, nears):
        sends.extend(group.values())
    for copy in sends:
        copy.wait_send()


def grouped(n_b, single, per_batch, n_exp, n_ten, cap, batches, plans, *refs):
    refs = list(refs)
    names, values = [], []
    for name in single:
        names.append(name)
        values.append(refs.pop(0))
    for name in per_batch:
        names.append(name)
        values.append([refs.pop(0) for _ in range(n_b)])
    kernel(n_exp, n_ten, cap, batches, plans, names, *values)


def fused(tokens, route_logit, expert_ids, w_gate, w_up, w_down):
    n_exp = lax.axis_size("expert")
    n_ten = lax.axis_size("tensor")
    tok, width = tokens.shape
    n_ff = w_gate.shape[2]
    cap = 5 * tok // (4 * n_exp)
    slots = n_exp * cap
    batches = cut(cap)
    made = [plan(width, rows) for _, rows in batches]
    plans = [chunks for chunks, _ in made]
    n_b, n_c = len(batches), len(plans[0])
    vmem, dma = pltpu.VMEM, pltpu.SemaphoreType.DMA
    scratch = {
        "tokens": vmem((tok, width), BF16),
        "logit": vmem((1, tok), F32),
        "ids": vmem((1, tok), jnp.int32),
        "wg": vmem((n_ten, width, n_ff), BF16),
        "wu": vmem((n_ten, width, n_ff), BF16),
        "wd": vmem((n_ten, n_ff, width), BF16),
        "in_sem": dma((3,)),
        "w_sem": dma((3, n_ten)),
    }
    for kind in ("d", "r"):
        scratch["s_" + kind] = dma((n_b, n_exp, n_c))
        scratch["r_" + kind] = dma((n_b, n_exp, n_c))
    for kind in ("cross", "side", "fwd", "far", "half", "near"):
        scratch["s_" + kind] = dma((n_b, n_c))
        scratch["r_" + kind] = dma((n_b, n_c))
    lists = {}
    for name in ("send_d", "recv_d", "send_r", "recv_r"):
        lists[name] = [vmem((n_exp, block, 128), BF16) for _, block in made]
    counts = [n_exp * rows for _, rows in batches]
    lists["x"] = [vmem((n_ten, n, width), BF16) for n in counts]
    for name in ("acc_g", "acc_u"):
        lists[name] = [vmem((n, n_ff), F32) for n in counts]
    lists["hidden"] = [vmem((n, n_ff), BF16) for n in counts]
    lists["combine"] = [vmem((tok, n), BF16) for n in counts]
    for name in ("far_out", "far_in", "far_own", "near_out", "near_in", "near_own"):
        lists[name] = [vmem((n, width), F32) for n in counts]
    for name in ("half_out", "half_in"):
        lists[name] = [vmem((n, width), BF16) for n in counts]
    single = ["tokens_in", "logit_in", "ids_in", "w_gate", "w_up", "w_down", "out"] + list(scratch)
    return pl.pallas_call(
        functools.partial(grouped, n_b, single, list(lists), n_exp, n_ten, cap, batches, plans),
        out_shape=jax.ShapeDtypeStruct((tok, width), BF16),
        in_specs=[pl.BlockSpec(memory_space=pl.ANY)] * 6,
        out_specs=pl.BlockSpec(memory_space=vmem),
        scratch_shapes=list(scratch.values()) + [ref for group in lists.values() for ref in group],
        compiler_params=pltpu.CompilerParams(
            collective_id=0, has_side_effects=True, vmem_limit_bytes=LIMIT
        ),
        cost_estimate=pl.CostEstimate(
            flops=6 * slots * n_ten * width * n_ff,
            bytes_accessed=6 * n_ten * width * n_ff,
            transcendentals=slots * n_ff,
        ),
    )(tokens, route_logit.reshape(1, tok), expert_ids.reshape(1, tok), w_gate, w_up, w_down)


def on_device(tokens, route_logit, expert_ids, w_gate, w_up, w_down):
    expert_count = lax.axis_size("expert")
    tok_rows, width_local = tokens.shape
    capacity = 5 * tok_rows // (4 * expert_count)
    if (
        lax.axis_size("tensor") == 4
        and capacity % 8 == 0
        and width_local % 128 == 0
        and w_gate.shape[2] % 256 == 0
        and expert_count <= 8
    ):
        return fused(tokens, route_logit, expert_ids, w_gate, w_up, w_down)
    slot_count = expert_count * capacity
    route = expert_ids[:, 0]
    one_hot = (route[:, None] == jnp.arange(expert_count, dtype=jnp.int32)[None, :]).astype(
        jnp.int32
    )
    earlier = jnp.cumsum(one_hot, axis=0) - one_hot
    position = jnp.sum(earlier * one_hot, axis=1)
    destination = route * capacity + position
    dispatch_map = (
        jnp.arange(slot_count, dtype=jnp.int32)[:, None] == destination[None, :]
    ).astype(jnp.bfloat16)
    factor = jax.nn.sigmoid(route_logit)
    scaled = (factor[:, None] * tokens.astype(jnp.float32)).astype(jnp.bfloat16)
    outgoing = jnp.dot(dispatch_map, scaled, preferred_element_type=jnp.float32).astype(
        jnp.bfloat16
    )
    outgoing = outgoing.reshape(expert_count, capacity, width_local)
    arrived = lax.all_to_all(outgoing, "expert", split_axis=0, concat_axis=0, tiled=True).reshape(
        slot_count, width_local
    )
    gate_local = w_gate[0]
    lift_local = w_up[0]
    down_local = w_down[0]
    piece = lax.all_gather(arrived, "tensor", axis=1, tiled=True)
    gate_val = jnp.dot(piece, gate_local, preferred_element_type=jnp.float32)
    lift_val = jnp.dot(piece, lift_local, preferred_element_type=jnp.float32)
    hidden = (jax.nn.silu(gate_val) * lift_val).astype(jnp.bfloat16)
    summed = lax.psum_scatter(
        lax.dot_general(
            down_local, hidden, (((0,), (1,)), ((), ())), preferred_element_type=jnp.float32
        ),
        "tensor",
        scatter_dimension=0,
        tiled=True,
    )
    expert_out = summed.astype(jnp.bfloat16).reshape(width_local, expert_count, capacity)
    returned = lax.all_to_all(
        expert_out, "expert", split_axis=1, concat_axis=1, tiled=True
    ).reshape(width_local, slot_count)
    mixed = lax.dot_general(
        dispatch_map, returned, (((0,), (1,)), ((), ())), preferred_element_type=jnp.float32
    )
    return mixed.astype(jnp.bfloat16)


def solution(mesh):
    return jax.shard_map(
        on_device,
        mesh=mesh,
        in_specs=(
            P("expert", "tensor"),
            P("expert"),
            P("expert", None),
            P("expert", None, "tensor"),
            P("expert", None, "tensor"),
            P("expert", "tensor", None),
        ),
        out_specs=P("expert", "tensor"),
        check_vma=False,
    )
```

```python
import functools

import jax
import jax.numpy as jnp
from jax import lax
from jax.experimental import pallas as pl
from jax.experimental.pallas import tpu as pltpu
from jax.sharding import PartitionSpec as P

MESH = pl.DeviceIdType.MESH
LIMIT = 63 * 1024 * 1024
F32 = jnp.float32
BF16 = jnp.bfloat16


def plan(width, cap):
    chunks, off, row = [], 0, 0
    while off < width:
        lanes = min(384 if width == 640 and off == 0 else 256, width - off)
        rows = -(-(cap * (lanes // 128)) // 16) * 16
        chunks.append((off, lanes, row, rows))
        off, row = off + lanes, row + rows
    return chunks, row


def pack(block, lanes, rows):
    parts = [block[:, i : i + 128] for i in range(0, lanes, 128)]
    spare = rows - block.shape[0] * len(parts)
    if spare:
        parts.append(jnp.zeros((spare, 128), F32))
    return jnp.concatenate(parts, axis=0) if len(parts) > 1 else parts[0]


def unpack(packed, lanes, cap):
    packed = packed.astype(F32)
    parts = [packed[i * cap : (i + 1) * cap] for i in range(lanes // 128)]
    return jnp.concatenate(parts, axis=1) if len(parts) > 1 else parts[0]


def cut(cap):
    return [(0, cap)]


def kernel(n_exp, n_ten, cap, batches, plans, names, *refs):
    r = dict(zip(names, refs))
    tokens, logit, ids = r["tokens"], r["logit"], r["ids"]
    wg, wu, wd, combine, out = r["wg"], r["wu"], r["wd"], r["combine"], r["out"]
    w_sem = r["w_sem"]
    g = lax.axis_index("expert")
    t = lax.axis_index("tensor")
    sib = t + 1 - 2 * lax.rem(t, 2)
    across = lax.rem(t + 2, 4)
    diag = lax.rem(sib + 2, 4)
    tok, width = tokens.shape
    n_ff = wg.shape[2]
    n_chunks = len(plans[0])
    tile = 512 if n_ff % 512 == 0 else 256
    order = list(range(1, n_exp))
    all_b = range(len(batches))

    small = [
        pltpu.make_async_copy(r[name + "_in"], r[name], r["in_sem"].at[i])
        for i, name in enumerate(("ids", "logit", "tokens"))
    ]
    for copy in small:
        copy.start()

    barrier = pltpu.get_barrier_semaphore()
    for k in order:
        pl.semaphore_signal(barrier, inc=1, device_id=(lax.rem(g + k, n_exp), t), device_id_type=MESH)
    for peer in (sib, across):
        pl.semaphore_signal(barrier, inc=1, device_id=(g, peer), device_id_type=MESH)

    w_loads, down_loads = [], []
    for i, s in enumerate((t, sib, across, diag)):
        rows_of = pl.ds(pl.multiple_of(s * width, 128), width)
        w_loads.append(pltpu.make_async_copy(r["w_gate"].at[0, rows_of], wg.at[s], w_sem.at[0, i]))
        w_loads.append(pltpu.make_async_copy(r["w_up"].at[0, rows_of], wu.at[s], w_sem.at[1, i]))
    for s in range(n_ten):
        down_loads.append(
            pltpu.make_async_copy(r["w_down"].at[0, :, pl.ds(s * width, width)], wd.at[s], w_sem.at[2, s])
        )

    small[0].wait()
    ids_row = ids[...]
    one_hot = lax.broadcasted_iota(jnp.int32, (n_exp, tok), 0) == ids_row
    older = lax.broadcasted_iota(jnp.int32, (tok, tok), 0)
    newer = lax.broadcasted_iota(jnp.int32, (tok, tok), 1)
    before = jnp.where(older < newer, 1.0, 0.0).astype(BF16)
    hot = jnp.where(one_hot, 1.0, 0.0)
    earlier = jnp.dot(hot.astype(BF16), before, preferred_element_type=F32)
    position = jnp.sum(earlier * hot, axis=0, keepdims=True)
    dest = ids_row.astype(F32) * float(cap) + position
    eye = older == newer
    dispatch = []
    for first, rows in batches:
        row = lax.broadcasted_iota(jnp.int32, (rows, tok), 0)
        slot = jnp.concatenate([row + (e * cap + first) for e in range(n_exp)], axis=0).astype(F32)
        dispatch.append(jnp.where(slot == dest, 1.0, 0.0).astype(BF16))
    small[1].wait()
    factor = jnp.sum(jnp.where(eye, jax.nn.sigmoid(logit[...]), 0.0), axis=1, keepdims=True)

    def exchange(b, c, kind):
        _, _, row, rows = plans[b][c]
        src, dst = r["send_" + kind][b], r["recv_" + kind][b]
        copies = []
        for k in order:
            e = lax.rem(g + k, n_exp)
            copies.append(
                pltpu.make_async_remote_copy(
                    src_ref=src.at[e, pl.ds(row, rows)],
                    dst_ref=dst.at[g, pl.ds(row, rows)],
                    send_sem=r["s_" + kind].at[b, k, c],
                    recv_sem=r["r_" + kind].at[b, k, c],
                    device_id=(e, t),
                    device_id_type=MESH,
                )
            )
        return copies

    def to_tensor(src, dst, kind, b, c, peer):
        return pltpu.make_async_remote_copy(
            src_ref=src,
            dst_ref=dst,
            send_sem=r["s_" + kind].at[b, c],
            recv_sem=r["r_" + kind].at[b, c],
            device_id=(g, peer),
            device_id_type=MESH,
        )

    def post(b, c, kind, values):
        _, lanes, row, rows = plans[b][c]
        n = batches[b][1]
        src, dst = r["send_" + kind][b], r["recv_" + kind][b]
        for e in range(n_exp):
            src[e, row : row + rows] = pack(values[e * n : (e + 1) * n], lanes, rows).astype(BF16)
        copies = exchange(b, c, kind)
        if kind == "d" and b == 0 and c == 0:
            pl.semaphore_wait(barrier, n_exp - 1 + 2)
        for copy in copies:
            copy.start()
        dst[g, row : row + rows] = src[g, row : row + rows]
        sends.extend(copies)
        return copies

    def collect(b, c, kind, copies):
        _, lanes, row, rows = plans[b][c]
        for copy in copies:
            copy.wait_recv()
        src = r["recv_" + kind][b]
        return jnp.concatenate(
            [unpack(src[e, row : row + rows], lanes, batches[b][1]) for e in range(n_exp)], axis=0
        ).astype(BF16)

    sends = []
    small[2].wait()
    for load in w_loads[:4]:
        load.start()
    scaled = (factor * tokens[...].astype(F32)).astype(BF16)
    dispatches = {}
    for b in all_b:
        for c in range(n_chunks):
            off, lanes, _, _ = plans[b][c]
            outgoing = jnp.dot(dispatch[b], scaled[:, off : off + lanes], preferred_element_type=F32)
            dispatches[b, c] = post(b, c, "d", outgoing)

    for load in w_loads[4:] + down_loads:
        load.start()

    dest_col = jnp.sum(jnp.where(eye, dest, 0.0), axis=1, keepdims=True)
    for b, (first, rows) in enumerate(batches):
        lane = lax.broadcasted_iota(jnp.int32, (1, n_exp * rows), 1)
        slot = lane + first
        for e in range(1, n_exp):
            slot = slot + jnp.where(lane >= e * rows, cap - rows, 0)
        combine[b][...] = jnp.where(slot.astype(F32) == dest_col, 1.0, 0.0).astype(BF16)

    crossing, sides, forwards = {}, {}, {}

    def gather(b, c):
        off, lanes, _, _ = plans[b][c]
        x = r["x"][b]
        x[t, :, off : off + lanes] = collect(b, c, "d", dispatches[b, c])
        part = x.at[t, :, pl.ds(off, lanes)]
        crossing[b, c] = to_tensor(part, part, "cross", b, c, across)
        sides[b, c] = to_tensor(part, part, "side", b, c, sib)
        crossing[b, c].start()
        sides[b, c].start()

    def forward(b, c):
        off, lanes, _, _ = plans[b][c]
        crossing[b, c].wait_recv()
        part = r["x"][b].at[across, :, pl.ds(off, lanes)]
        forwards[b, c] = to_tensor(part, part, "fwd", b, c, sib)
        forwards[b, c].start()

    def project(b, c, one, two, begin, end):
        off, lanes, _, _ = plans[b][c]
        x, acc_g, acc_u, hidden = r["x"][b], r["acc_g"][b], r["acc_u"][b], r["hidden"][b]
        feats = slice(off, off + lanes)
        rows_in = jnp.concatenate([x[one, :, feats], x[two, :, feats]], axis=1)
        for n in range(0, n_ff, tile):
            cols = slice(n, n + tile)

            def product(w):
                w_in = jnp.concatenate([w[one, feats, cols], w[two, feats, cols]], axis=0)
                return jnp.dot(rows_in, w_in, preferred_element_type=F32)

            gate, lift = product(wg), product(wu)
            if not begin:
                gate = gate + acc_g[:, cols]
                lift = lift + acc_u[:, cols]
            if end:
                hidden[:, cols] = ((0.5 * gate) * (1.0 + jnp.tanh(0.5 * gate)) * lift).astype(BF16)
            else:
                acc_g[:, cols] = gate
                acc_u[:, cols] = lift

    def near_pair(b, c):
        sides[b, c].wait_recv()
        project(b, c, t, sib, c == 0, False)

    def far_pair(b, c):
        forwards[b, c].wait_recv()
        project(b, c, across, diag, False, c == n_chunks - 1)

    back = list(range(n_chunks))[::-1]
    fars, halves, nears, returns = {}, {}, {}, {}

    def partials(b, one, two, c):
        off, lanes, _, _ = plans[b][c]
        rows_in, part = r["hidden"][b][...], slice(off, off + lanes)
        if lanes % 256:
            both = jnp.dot(
                rows_in,
                jnp.concatenate([wd[one, :, part], wd[two, :, part]], axis=1),
                preferred_element_type=F32,
            )
            return (lambda: both[:, :lanes]), (lambda: both[:, lanes:])
        return tuple(
            functools.partial(jnp.dot, rows_in, wd[s, :, part], preferred_element_type=F32) for s in (one, two)
        )

    def start_far(b, c):
        off, lanes, _, _ = plans[b][c]
        part = pl.ds(off, lanes)
        theirs, mine = partials(b, diag, across, c)
        r["far_out"][b][:, off : off + lanes] = theirs()
        fars[b, c] = to_tensor(r["far_out"][b].at[:, part], r["far_in"][b].at[:, part], "far", b, c, sib)
        fars[b, c].start()
        r["far_own"][b][:, off : off + lanes] = mine()

    def start_half(b, c):
        off, lanes, _, _ = plans[b][c]
        part, lane = pl.ds(off, lanes), slice(off, off + lanes)
        fars[b, c].wait_recv()
        r["half_out"][b][:, lane] = (r["far_own"][b][:, lane] + r["far_in"][b][:, lane]).astype(BF16)
        halves[b, c] = to_tensor(r["half_out"][b].at[:, part], r["half_in"][b].at[:, part], "half", b, c, across)
        halves[b, c].start()

    def far_side(b):
        start_far(b, back[0])
        for i, c in enumerate(back):
            if i + 1 < n_chunks:
                start_far(b, back[i + 1])
            start_half(b, c)

    def near_side(b):
        for c in back:
            off, lanes, _, _ = plans[b][c]
            part = pl.ds(off, lanes)
            theirs, mine = partials(b, sib, t, c)
            r["near_out"][b][:, off : off + lanes] = theirs()
            nears[b, c] = to_tensor(r["near_out"][b].at[:, part], r["near_in"][b].at[:, part], "near", b, c, sib)
            nears[b, c].start()
            r["near_own"][b][:, off : off + lanes] = mine()

    def give_back(b, c):
        off, lanes, _, _ = plans[b][c]
        lane = slice(off, off + lanes)
        nears[b, c].wait_recv()
        halves[b, c].wait_recv()
        total = (
            r["near_own"][b][:, lane] + r["near_in"][b][:, lane] + r["half_in"][b][:, lane].astype(F32)
        )
        returns[b, c] = post(b, c, "r", total)

    last = n_chunks - 1

    gather(0, 0)
    for load in w_loads[:4]:
        load.wait()
    near_pair(0, 0)
    for c in range(1, n_chunks):
        gather(0, c)
        if c == 1:
            forward(0, 0)
        if c < last:
            near_pair(0, c)
    for load in w_loads[4:]:
        load.wait()
    far_pair(0, 0)
    for c in range(1, last):
        forward(0, c)
    near_pair(0, last)
    forward(0, last)
    for c in range(1, n_chunks):
        far_pair(0, c)
    for load in down_loads:
        load.wait()
    far_side(0)
    near_side(0)
    for c in back:
        give_back(0, c)

    for c in back:
        off, lanes, _, _ = plans[0][c]
        mixed = None
        for b in all_b:
            term = jnp.dot(combine[b][...], collect(b, c, "r", returns[b, c]), preferred_element_type=F32)
            mixed = term if mixed is None else mixed + term
        out[:, off : off + lanes] = mixed.astype(BF16)

    for group in (crossing, sides, forwards, fars, halves, nears):
        sends.extend(group.values())
    for copy in sends:
        copy.wait_send()


def grouped(n_b, single, per_batch, n_exp, n_ten, cap, batches, plans, *refs):
    refs = list(refs)
    names, values = [], []
    for name in single:
        names.append(name)
        values.append(refs.pop(0))
    for name in per_batch:
        names.append(name)
        values.append([refs.pop(0) for _ in range(n_b)])
    kernel(n_exp, n_ten, cap, batches, plans, names, *values)


def fused(tokens, route_logit, expert_ids, w_gate, w_up, w_down):
    n_exp = lax.axis_size("expert")
    n_ten = lax.axis_size("tensor")
    tok, width = tokens.shape
    n_ff = w_gate.shape[2]
    cap = 5 * tok // (4 * n_exp)
    slots = n_exp * cap
    batches = cut(cap)
    made = [plan(width, rows) for _, rows in batches]
    plans = [chunks for chunks, _ in made]
    n_b, n_c = len(batches), len(plans[0])
    vmem, dma = pltpu.VMEM, pltpu.SemaphoreType.DMA
    scratch = {
        "tokens": vmem((tok, width), BF16),
        "logit": vmem((1, tok), F32),
        "ids": vmem((1, tok), jnp.int32),
        "wg": vmem((n_ten, width, n_ff), BF16),
        "wu": vmem((n_ten, width, n_ff), BF16),
        "wd": vmem((n_ten, n_ff, width), BF16),
        "in_sem": dma((3,)),
        "w_sem": dma((3, n_ten)),
    }
    for kind in ("d", "r"):
        scratch["s_" + kind] = dma((n_b, n_exp, n_c))
        scratch["r_" + kind] = dma((n_b, n_exp, n_c))
    for kind in ("cross", "side", "fwd", "far", "half", "near"):
        scratch["s_" + kind] = dma((n_b, n_c))
        scratch["r_" + kind] = dma((n_b, n_c))
    lists = {}
    for name in ("send_d", "recv_d", "send_r", "recv_r"):
        lists[name] = [vmem((n_exp, block, 128), BF16) for _, block in made]
    counts = [n_exp * rows for _, rows in batches]
    lists["x"] = [vmem((n_ten, n, width), BF16) for n in counts]
    for name in ("acc_g", "acc_u"):
        lists[name] = [vmem((n, n_ff), F32) for n in counts]
    lists["hidden"] = [vmem((n, n_ff), BF16) for n in counts]
    lists["combine"] = [vmem((tok, n), BF16) for n in counts]
    for name in ("far_out", "far_in", "far_own", "near_out", "near_in", "near_own"):
        lists[name] = [vmem((n, width), F32) for n in counts]
    for name in ("half_out", "half_in"):
        lists[name] = [vmem((n, width), BF16) for n in counts]
    single = ["tokens_in", "logit_in", "ids_in", "w_gate", "w_up", "w_down", "out"] + list(scratch)
    return pl.pallas_call(
        functools.partial(grouped, n_b, single, list(lists), n_exp, n_ten, cap, batches, plans),
        out_shape=jax.ShapeDtypeStruct((tok, width), BF16),
        in_specs=[pl.BlockSpec(memory_space=pl.ANY)] * 6,
        out_specs=pl.BlockSpec(memory_space=vmem),
        scratch_shapes=list(scratch.values()) + [ref for group in lists.values() for ref in group],
        compiler_params=pltpu.CompilerParams(
            collective_id=0, has_side_effects=True, vmem_limit_bytes=LIMIT
        ),
        cost_estimate=pl.CostEstimate(
            flops=6 * slots * n_ten * width * n_ff,
            bytes_accessed=6 * n_ten * width * n_ff,
            transcendentals=slots * n_ff,
        ),
    )(tokens, route_logit.reshape(1, tok), expert_ids.reshape(1, tok), w_gate, w_up, w_down)


def on_device(tokens, route_logit, expert_ids, w_gate, w_up, w_down):
    expert_count = lax.axis_size("expert")
    tok_rows, width_local = tokens.shape
    capacity = 5 * tok_rows // (4 * expert_count)
    if (
        lax.axis_size("tensor") == 4
        and capacity % 8 == 0
        and width_local % 128 == 0
        and w_gate.shape[2] % 256 == 0
        and expert_count <= 8
    ):
        return fused(tokens, route_logit, expert_ids, w_gate, w_up, w_down)
    slot_count = expert_count * capacity
    route = expert_ids[:, 0]
    one_hot = (route[:, None] == jnp.arange(expert_count, dtype=jnp.int32)[None, :]).astype(
        jnp.int32
    )
    earlier = jnp.cumsum(one_hot, axis=0) - one_hot
    position = jnp.sum(earlier * one_hot, axis=1)
    destination = route * capacity + position
    dispatch_map = (
        jnp.arange(slot_count, dtype=jnp.int32)[:, None] == destination[None, :]
    ).astype(jnp.bfloat16)
    factor = jax.nn.sigmoid(route_logit)
    scaled = (factor[:, None] * tokens.astype(jnp.float32)).astype(jnp.bfloat16)
    outgoing = jnp.dot(dispatch_map, scaled, preferred_element_type=jnp.float32).astype(
        jnp.bfloat16
    )
    outgoing = outgoing.reshape(expert_count, capacity, width_local)
    arrived = lax.all_to_all(outgoing, "expert", split_axis=0, concat_axis=0, tiled=True).reshape(
        slot_count, width_local
    )
    gate_local = w_gate[0]
    lift_local = w_up[0]
    down_local = w_down[0]
    piece = lax.all_gather(arrived, "tensor", axis=1, tiled=True)
    gate_val = jnp.dot(piece, gate_local, preferred_element_type=jnp.float32)
    lift_val = jnp.dot(piece, lift_local, preferred_element_type=jnp.float32)
    hidden = (jax.nn.silu(gate_val) * lift_val).astype(jnp.bfloat16)
    summed = lax.psum_scatter(
        lax.dot_general(
            down_local, hidden, (((0,), (1,)), ((), ())), preferred_element_type=jnp.float32
        ),
        "tensor",
        scatter_dimension=0,
        tiled=True,
    )
    expert_out = summed.astype(jnp.bfloat16).reshape(width_local, expert_count, capacity)
    returned = lax.all_to_all(
        expert_out, "expert", split_axis=1, concat_axis=1, tiled=True
    ).reshape(width_local, slot_count)
    mixed = lax.dot_general(
        dispatch_map, returned, (((0,), (1,)), ((), ())), preferred_element_type=jnp.float32
    )
    return mixed.astype(jnp.bfloat16)


def solution(mesh):
    return jax.shard_map(
        on_device,
        mesh=mesh,
        in_specs=(
            P("expert", "tensor"),
            P("expert"),
            P("expert", None),
            P("expert", None, "tensor"),
            P("expert", None, "tensor"),
            P("expert", "tensor", None),
        ),
        out_specs=P("expert", "tensor"),
        check_vma=False,
    )
```

```python
import functools

import jax
import jax.numpy as jnp
from jax import lax
from jax.experimental import pallas as pl
from jax.experimental.pallas import tpu as pltpu
from jax.sharding import PartitionSpec as P

MESH = pl.DeviceIdType.MESH
LIMIT = 63 * 1024 * 1024
F32 = jnp.float32
BF16 = jnp.bfloat16


def plan(width, cap):
    chunks, off, row = [], 0, 0
    while off < width:
        lanes = min(256, width - off)
        rows = -(-(cap * (lanes // 128)) // 16) * 16
        chunks.append((off, lanes, row, rows))
        off, row = off + lanes, row + rows
    return chunks, row


def pack(block, lanes, rows):
    parts = [block[:, i : i + 128] for i in range(0, lanes, 128)]
    spare = rows - block.shape[0] * len(parts)
    if spare:
        parts.append(jnp.zeros((spare, 128), F32))
    return jnp.concatenate(parts, axis=0) if len(parts) > 1 else parts[0]


def unpack(packed, lanes, cap):
    packed = packed.astype(F32)
    parts = [packed[i * cap : (i + 1) * cap] for i in range(lanes // 128)]
    return jnp.concatenate(parts, axis=1) if len(parts) > 1 else parts[0]


def cut(cap):
    first = 24 if cap == 40 else cap
    return [(0, first)] + ([(first, cap - first)] if cap > first else [])


def kernel(n_exp, n_ten, cap, batches, plans, names, *refs):
    r = dict(zip(names, refs))
    tokens, logit, ids = r["tokens"], r["logit"], r["ids"]
    wg, wu, wd, out = r["wg"], r["wu"], r["wd"], r["out"]
    w_sem = r["w_sem"]
    g = lax.axis_index("expert")
    t = lax.axis_index("tensor")
    sib = t + 1 - 2 * lax.rem(t, 2)
    across = lax.rem(t + 2, 4)
    diag = lax.rem(sib + 2, 4)
    tok, width = tokens.shape
    n_ff = wg.shape[2]
    n_chunks = len(plans[0])
    tile = 512 if n_ff % 512 == 0 else 256
    order = list(range(1, n_exp))
    all_b = range(len(batches))

    small = [
        pltpu.make_async_copy(r[name + "_in"], r[name], r["in_sem"].at[i])
        for i, name in enumerate(("ids", "logit", "tokens"))
    ]
    for copy in small:
        copy.start()

    barrier = pltpu.get_barrier_semaphore()
    for k in order:
        pl.semaphore_signal(barrier, inc=1, device_id=(lax.rem(g + k, n_exp), t), device_id_type=MESH)
    for peer in (sib, across):
        pl.semaphore_signal(barrier, inc=1, device_id=(g, peer), device_id_type=MESH)

    w_loads, down_loads = [], []
    for i, s in enumerate((t, sib, across, diag)):
        rows_of = pl.ds(pl.multiple_of(s * width, 128), width)
        w_loads.append(pltpu.make_async_copy(r["w_gate"].at[0, rows_of], wg.at[s], w_sem.at[0, i]))
        w_loads.append(pltpu.make_async_copy(r["w_up"].at[0, rows_of], wu.at[s], w_sem.at[1, i]))
    for s in range(n_ten):
        down_loads.append(
            pltpu.make_async_copy(r["w_down"].at[0, :, pl.ds(s * width, width)], wd.at[s], w_sem.at[2, s])
        )

    small[0].wait()
    ids_row = ids[...]
    one_hot = lax.broadcasted_iota(jnp.int32, (n_exp, tok), 0) == ids_row
    older = lax.broadcasted_iota(jnp.int32, (tok, tok), 0)
    newer = lax.broadcasted_iota(jnp.int32, (tok, tok), 1)
    before = jnp.where(older < newer, 1.0, 0.0).astype(BF16)
    hot = jnp.where(one_hot, 1.0, 0.0)
    earlier = jnp.dot(hot.astype(BF16), before, preferred_element_type=F32)
    position = jnp.sum(earlier * hot, axis=0, keepdims=True)
    dest = ids_row.astype(F32) * float(cap) + position
    eye = older == newer
    bases = [n_exp * first for first, _ in batches]
    parts = []
    for first, rows in batches:
        row = lax.broadcasted_iota(jnp.int32, (rows, tok), 0)
        parts += [row + (e * cap + first) for e in range(n_exp)]
    slot = jnp.concatenate(parts, axis=0).astype(F32)
    dispatch = jnp.where(slot == dest, 1.0, 0.0).astype(BF16)
    small[1].wait()
    factor = jnp.sum(jnp.where(eye, jax.nn.sigmoid(logit[...]), 0.0), axis=1, keepdims=True)

    def exchange(b, c, kind):
        _, _, row, rows = plans[b][c]
        src, dst = r["send_" + kind][b], r["recv_" + kind][b]
        copies = []
        for k in order:
            e = lax.rem(g + k, n_exp)
            copies.append(
                pltpu.make_async_remote_copy(
                    src_ref=src.at[e, pl.ds(row, rows)],
                    dst_ref=dst.at[g, pl.ds(row, rows)],
                    send_sem=r["s_" + kind].at[b, k, c],
                    recv_sem=r["r_" + kind].at[b, k, c],
                    device_id=(e, t),
                    device_id_type=MESH,
                )
            )
        return copies

    def to_tensor(src, dst, kind, b, c, peer):
        return pltpu.make_async_remote_copy(
            src_ref=src,
            dst_ref=dst,
            send_sem=r["s_" + kind].at[b, c],
            recv_sem=r["r_" + kind].at[b, c],
            device_id=(g, peer),
            device_id_type=MESH,
        )

    def post(b, c, kind, values):
        _, lanes, row, rows = plans[b][c]
        n = batches[b][1]
        src, dst = r["send_" + kind][b], r["recv_" + kind][b]
        for e in range(n_exp):
            src[e, row : row + rows] = pack(values[e * n : (e + 1) * n], lanes, rows).astype(BF16)
        copies = exchange(b, c, kind)
        if kind == "d" and b == 0 and c == 0:
            pl.semaphore_wait(barrier, n_exp - 1 + 2)
        for copy in copies:
            copy.start()
        dst[g, row : row + rows] = src[g, row : row + rows]
        sends.extend(copies)
        return copies

    def collect(b, c, kind, copies):
        _, lanes, row, rows = plans[b][c]
        for copy in copies:
            copy.wait_recv()
        src = r["recv_" + kind][b]
        return jnp.concatenate(
            [unpack(src[e, row : row + rows], lanes, batches[b][1]) for e in range(n_exp)], axis=0
        ).astype(BF16)

    sends = []
    small[2].wait()
    for load in w_loads[:4]:
        load.start()
    scaled = (factor * tokens[...].astype(F32)).astype(BF16)
    dispatches = {}
    for c in range(n_chunks):
        off, lanes, _, _ = plans[0][c]
        outgoing = jnp.dot(dispatch, scaled[:, off : off + lanes], preferred_element_type=F32)
        for b in all_b:
            dispatches[b, c] = post(b, c, "d", outgoing[bases[b] : bases[b] + n_exp * batches[b][1]])

    for load in w_loads[4:] + down_loads:
        load.start()

    dest_col = jnp.sum(jnp.where(eye, dest, 0.0), axis=1, keepdims=True)
    for b, (first, rows) in enumerate(batches):
        lane = lax.broadcasted_iota(jnp.int32, (1, n_exp * rows), 1)
        slot = lane + first
        for e in range(1, n_exp):
            slot = slot + jnp.where(lane >= e * rows, cap - rows, 0)
        r["combine"][b][...] = jnp.where(slot.astype(F32) == dest_col, 1.0, 0.0).astype(BF16)

    crossing, sides, forwards = {}, {}, {}

    x, acc_g, acc_u, hidden = r["x"], r["acc_g"], r["acc_u"], r["hidden"]

    def rows_of_batch(b):
        return pl.ds(bases[b], n_exp * batches[b][1])

    def gather(b, c):
        off, lanes, _, _ = plans[b][c]
        here = slice(bases[b], bases[b] + n_exp * batches[b][1])
        x[t, here, off : off + lanes] = collect(b, c, "d", dispatches[b, c])
        part = x.at[t, rows_of_batch(b), pl.ds(off, lanes)]
        crossing[b, c] = to_tensor(part, part, "cross", b, c, across)
        sides[b, c] = to_tensor(part, part, "side", b, c, sib)
        crossing[b, c].start()
        sides[b, c].start()

    def forward(b, c):
        off, lanes, _, _ = plans[b][c]
        crossing[b, c].wait_recv()
        part = x.at[across, rows_of_batch(b), pl.ds(off, lanes)]
        forwards[b, c] = to_tensor(part, part, "fwd", b, c, sib)
        forwards[b, c].start()

    def project(c, one, two, begin, end, n):
        off, lanes, _, _ = plans[0][c]
        feats, cols = slice(off, off + lanes), slice(n, n + tile)
        rows_in = jnp.concatenate([x[one, :, feats], x[two, :, feats]], axis=1)

        def product(w):
            w_in = jnp.concatenate([w[one, feats, cols], w[two, feats, cols]], axis=0)
            return jnp.dot(rows_in, w_in, preferred_element_type=F32)

        gate, lift = product(wg), product(wu)
        if not begin:
            gate = gate + acc_g[:, cols]
            lift = lift + acc_u[:, cols]
        if end:
            hidden[:, cols] = ((0.5 * gate) * (1.0 + jnp.tanh(0.5 * gate)) * lift).astype(BF16)
        else:
            acc_g[:, cols] = gate
            acc_u[:, cols] = lift

    def near_pair(c, between=()):
        for b in all_b:
            sides[b, c].wait_recv()
        between = list(between)
        for n in range(0, n_ff, tile):
            project(c, t, sib, c == 0, False, n)
            if between:
                step, at_b, at_c = between.pop(0)
                step(at_b, at_c)
        for step, at_b, at_c in between:
            step(at_b, at_c)

    def far_pair(c):
        for b in all_b:
            forwards[b, c].wait_recv()
        for n in range(0, n_ff, tile):
            project(c, across, diag, False, c == n_chunks - 1, n)

    back = list(range(n_chunks))[::-1]
    fars, halves, nears, returns = {}, {}, {}, {}

    def partials(one, two, c):
        off, lanes, _, _ = plans[0][c]
        rows_in, part = hidden[...], slice(off, off + lanes)
        if lanes % 256:
            both = jnp.dot(
                rows_in,
                jnp.concatenate([wd[one, :, part], wd[two, :, part]], axis=1),
                preferred_element_type=F32,
            )
            return (lambda: both[:, :lanes]), (lambda: both[:, lanes:])
        return tuple(
            functools.partial(jnp.dot, rows_in, wd[s, :, part], preferred_element_type=F32) for s in (one, two)
        )

    def start_far(c):
        off, lanes, _, _ = plans[0][c]
        part = pl.ds(off, lanes)
        theirs, mine = partials(diag, across, c)
        r["far_out"][:, off : off + lanes] = theirs()
        fars[c] = to_tensor(r["far_out"].at[:, part], r["far_in"].at[:, part], "far", 0, c, sib)
        fars[c].start()
        r["far_own"][:, off : off + lanes] = mine()

    def start_half(c):
        off, lanes, _, _ = plans[0][c]
        part, lane = pl.ds(off, lanes), slice(off, off + lanes)
        fars[c].wait_recv()
        for b in all_b:
            here = slice(bases[b], bases[b] + n_exp * batches[b][1])
            r["half_out"][here, lane] = (r["far_own"][here, lane] + r["far_in"][here, lane]).astype(BF16)
            halves[b, c] = to_tensor(
                r["half_out"].at[rows_of_batch(b), part], r["half_in"].at[rows_of_batch(b), part], "half", b, c, across
            )
            halves[b, c].start()

    def far_side():
        start_far(back[0])
        for i, c in enumerate(back):
            if i + 1 < n_chunks:
                start_far(back[i + 1])
            start_half(c)

    def near_side():
        for c in back:
            off, lanes, _, _ = plans[0][c]
            part = pl.ds(off, lanes)
            theirs, mine = partials(sib, t, c)
            r["near_out"][:, off : off + lanes] = theirs()
            nears[c] = to_tensor(r["near_out"].at[:, part], r["near_in"].at[:, part], "near", 0, c, sib)
            nears[c].start()
            r["near_own"][:, off : off + lanes] = mine()

    def give_back(c):
        off, lanes, _, _ = plans[0][c]
        lane = slice(off, off + lanes)
        nears[c].wait_recv()
        for b in all_b:
            here = slice(bases[b], bases[b] + n_exp * batches[b][1])
            halves[b, c].wait_recv()
            total = r["near_own"][here, lane] + r["near_in"][here, lane] + r["half_in"][here, lane].astype(F32)
            returns[b, c] = post(b, c, "r", total)

    last = n_chunks - 1

    for b in all_b:
        gather(b, 0)
    for load in w_loads[:4]:
        load.wait()
    meanwhile = []
    for b in all_b:
        meanwhile += [(forward, b, 0), (gather, b, 1)]
    near_pair(0, meanwhile[1:2])
    for step, b, c in meanwhile[:1] + meanwhile[2:]:
        step(b, c)
    for load in w_loads[4:]:
        load.wait()
    far_pair(0)
    for c in range(1, n_chunks):
        if c < last:
            for b in all_b:
                gather(b, c + 1)
        steps = [(forward, b, c) for b in all_b]
        if c < last:
            forward(0, c)
            steps = steps[1:]
        near_pair(c, steps)
        if c > 1:
            far_pair(c - 1)
    far_pair(last)
    for load in down_loads:
        load.wait()
    far_side()
    near_side()
    for c in back:
        give_back(c)

    for c in back:
        off, lanes, _, _ = plans[0][c]
        mixed = None
        for b in all_b:
            term = jnp.dot(r["combine"][b][...], collect(b, c, "r", returns[b, c]), preferred_element_type=F32)
            mixed = term if mixed is None else mixed + term
        out[:, off : off + lanes] = mixed.astype(BF16)

    for group in (crossing, sides, forwards, fars, halves, nears):
        sends.extend(group.values())
    for copy in sends:
        copy.wait_send()


def grouped(n_b, single, per_batch, n_exp, n_ten, cap, batches, plans, *refs):
    refs = list(refs)
    names, values = [], []
    for name in single:
        names.append(name)
        values.append(refs.pop(0))
    for name in per_batch:
        names.append(name)
        values.append([refs.pop(0) for _ in range(n_b)])
    kernel(n_exp, n_ten, cap, batches, plans, names, *values)


def fused(tokens, route_logit, expert_ids, w_gate, w_up, w_down):
    n_exp = lax.axis_size("expert")
    n_ten = lax.axis_size("tensor")
    tok, width = tokens.shape
    n_ff = w_gate.shape[2]
    cap = 5 * tok // (4 * n_exp)
    slots = n_exp * cap
    batches = cut(cap)
    made = [plan(width, rows) for _, rows in batches]
    plans = [chunks for chunks, _ in made]
    n_b, n_c = len(batches), len(plans[0])
    vmem, dma = pltpu.VMEM, pltpu.SemaphoreType.DMA
    scratch = {
        "tokens": vmem((tok, width), BF16),
        "logit": vmem((1, tok), F32),
        "ids": vmem((1, tok), jnp.int32),
        "wg": vmem((n_ten, width, n_ff), BF16),
        "wu": vmem((n_ten, width, n_ff), BF16),
        "wd": vmem((n_ten, n_ff, width), BF16),
        "in_sem": dma((3,)),
        "w_sem": dma((3, n_ten)),
    }
    for kind in ("d", "r"):
        scratch["s_" + kind] = dma((n_b, n_exp, n_c))
        scratch["r_" + kind] = dma((n_b, n_exp, n_c))
    for kind in ("cross", "side", "fwd", "far", "half", "near"):
        scratch["s_" + kind] = dma((n_b, n_c))
        scratch["r_" + kind] = dma((n_b, n_c))
    lists = {}
    for name in ("send_d", "recv_d", "send_r", "recv_r"):
        lists[name] = [vmem((n_exp, block, 128), BF16) for _, block in made]
    lists["combine"] = [vmem((tok, n_exp * rows), BF16) for _, rows in batches]
    scratch["x"] = vmem((n_ten, slots, width), BF16)
    scratch["acc_g"] = scratch["acc_u"] = vmem((slots, n_ff), F32)
    scratch["hidden"] = vmem((slots, n_ff), BF16)
    for name in ("far_out", "far_in", "far_own", "near_out", "near_in", "near_own"):
        scratch[name] = vmem((slots, width), F32)
    scratch["half_out"] = scratch["half_in"] = vmem((slots, width), BF16)
    single = ["tokens_in", "logit_in", "ids_in", "w_gate", "w_up", "w_down", "out"] + list(scratch)
    return pl.pallas_call(
        functools.partial(grouped, n_b, single, list(lists), n_exp, n_ten, cap, batches, plans),
        out_shape=jax.ShapeDtypeStruct((tok, width), BF16),
        in_specs=[pl.BlockSpec(memory_space=pl.ANY)] * 6,
        out_specs=pl.BlockSpec(memory_space=vmem),
        scratch_shapes=list(scratch.values()) + [ref for group in lists.values() for ref in group],
        compiler_params=pltpu.CompilerParams(
            collective_id=0, has_side_effects=True, vmem_limit_bytes=LIMIT
        ),
        cost_estimate=pl.CostEstimate(
            flops=6 * slots * n_ten * width * n_ff,
            bytes_accessed=6 * n_ten * width * n_ff,
            transcendentals=slots * n_ff,
        ),
    )(tokens, route_logit.reshape(1, tok), expert_ids.reshape(1, tok), w_gate, w_up, w_down)


def on_device(tokens, route_logit, expert_ids, w_gate, w_up, w_down):
    expert_count = lax.axis_size("expert")
    tok_rows, width_local = tokens.shape
    capacity = 5 * tok_rows // (4 * expert_count)
    if (
        lax.axis_size("tensor") == 4
        and capacity % 8 == 0
        and width_local % 128 == 0
        and w_gate.shape[2] % 256 == 0
        and expert_count <= 8
    ):
        return fused(tokens, route_logit, expert_ids, w_gate, w_up, w_down)
    slot_count = expert_count * capacity
    route = expert_ids[:, 0]
    one_hot = (route[:, None] == jnp.arange(expert_count, dtype=jnp.int32)[None, :]).astype(
        jnp.int32
    )
    earlier = jnp.cumsum(one_hot, axis=0) - one_hot
    position = jnp.sum(earlier * one_hot, axis=1)
    destination = route * capacity + position
    dispatch_map = (
        jnp.arange(slot_count, dtype=jnp.int32)[:, None] == destination[None, :]
    ).astype(jnp.bfloat16)
    factor = jax.nn.sigmoid(route_logit)
    scaled = (factor[:, None] * tokens.astype(jnp.float32)).astype(jnp.bfloat16)
    outgoing = jnp.dot(dispatch_map, scaled, preferred_element_type=jnp.float32).astype(
        jnp.bfloat16
    )
    outgoing = outgoing.reshape(expert_count, capacity, width_local)
    arrived = lax.all_to_all(outgoing, "expert", split_axis=0, concat_axis=0, tiled=True).reshape(
        slot_count, width_local
    )
    gate_local = w_gate[0]
    lift_local = w_up[0]
    down_local = w_down[0]
    piece = lax.all_gather(arrived, "tensor", axis=1, tiled=True)
    gate_val = jnp.dot(piece, gate_local, preferred_element_type=jnp.float32)
    lift_val = jnp.dot(piece, lift_local, preferred_element_type=jnp.float32)
    hidden = (jax.nn.silu(gate_val) * lift_val).astype(jnp.bfloat16)
    summed = lax.psum_scatter(
        lax.dot_general(
            down_local, hidden, (((0,), (1,)), ((), ())), preferred_element_type=jnp.float32
        ),
        "tensor",
        scatter_dimension=0,
        tiled=True,
    )
    expert_out = summed.astype(jnp.bfloat16).reshape(width_local, expert_count, capacity)
    returned = lax.all_to_all(
        expert_out, "expert", split_axis=1, concat_axis=1, tiled=True
    ).reshape(width_local, slot_count)
    mixed = lax.dot_general(
        dispatch_map, returned, (((0,), (1,)), ((), ())), preferred_element_type=jnp.float32
    )
    return mixed.astype(jnp.bfloat16)


def solution(mesh):
    return jax.shard_map(
        on_device,
        mesh=mesh,
        in_specs=(
            P("expert", "tensor"),
            P("expert"),
            P("expert", None),
            P("expert", None, "tensor"),
            P("expert", None, "tensor"),
            P("expert", "tensor", None),
        ),
        out_specs=P("expert", "tensor"),
        check_vma=False,
    )
```

```python
import functools

import jax
import jax.numpy as jnp
from jax import lax
from jax.experimental import pallas as pl
from jax.experimental.pallas import tpu as pltpu
from jax.sharding import PartitionSpec as P

MESH = pl.DeviceIdType.MESH
LIMIT = 63 * 1024 * 1024
F32 = jnp.float32
BF16 = jnp.bfloat16


def plan(width, cap):
    chunks, off, row = [], 0, 0
    while off < width:
        lanes = min(256, width - off)
        rows = -(-(cap * (lanes // 128)) // 16) * 16
        chunks.append((off, lanes, row, rows))
        off, row = off + lanes, row + rows
    return chunks, row


def pack(block, lanes, rows):
    parts = [block[:, i : i + 128] for i in range(0, lanes, 128)]
    spare = rows - block.shape[0] * len(parts)
    if spare:
        parts.append(jnp.zeros((spare, 128), F32))
    return jnp.concatenate(parts, axis=0) if len(parts) > 1 else parts[0]


def unpack(packed, lanes, cap):
    packed = packed.astype(F32)
    parts = [packed[i * cap : (i + 1) * cap] for i in range(lanes // 128)]
    return jnp.concatenate(parts, axis=1) if len(parts) > 1 else parts[0]


def cut(cap):
    return [(0, cap)]


def kernel(n_exp, n_ten, cap, batches, plans, names, *refs):
    r = dict(zip(names, refs))
    tokens, logit, ids = r["tokens"], r["logit"], r["ids"]
    wg, wu, wd, combine, out = r["wg"], r["wu"], r["wd"], r["combine"], r["out"]
    w_sem = r["w_sem"]
    g = lax.axis_index("expert")
    t = lax.axis_index("tensor")
    sib = t + 1 - 2 * lax.rem(t, 2)
    across = lax.rem(t + 2, 4)
    diag = lax.rem(sib + 2, 4)
    tok, width = tokens.shape
    n_ff = wg.shape[2]
    n_chunks = len(plans[0])
    tile = 512 if n_ff % 512 == 0 else 256
    order = list(range(1, n_exp))
    all_b = range(len(batches))

    small = [
        pltpu.make_async_copy(r[name + "_in"], r[name], r["in_sem"].at[i])
        for i, name in enumerate(("ids", "logit", "tokens"))
    ]
    for copy in small:
        copy.start()

    barrier = pltpu.get_barrier_semaphore()
    for k in order:
        pl.semaphore_signal(barrier, inc=1, device_id=(lax.rem(g + k, n_exp), t), device_id_type=MESH)
    for peer in (sib, across):
        pl.semaphore_signal(barrier, inc=1, device_id=(g, peer), device_id_type=MESH)

    w_loads, down_loads = [], []
    for i, s in enumerate((t, sib, across, diag)):
        rows_of = pl.ds(pl.multiple_of(s * width, 128), width)
        w_loads.append(pltpu.make_async_copy(r["w_gate"].at[0, rows_of], wg.at[s], w_sem.at[0, i]))
        w_loads.append(pltpu.make_async_copy(r["w_up"].at[0, rows_of], wu.at[s], w_sem.at[1, i]))
    for s in range(n_ten):
        down_loads.append(
            pltpu.make_async_copy(r["w_down"].at[0, :, pl.ds(s * width, width)], wd.at[s], w_sem.at[2, s])
        )

    small[0].wait()
    ids_row = ids[...]
    one_hot = lax.broadcasted_iota(jnp.int32, (n_exp, tok), 0) == ids_row
    older = lax.broadcasted_iota(jnp.int32, (tok, tok), 0)
    newer = lax.broadcasted_iota(jnp.int32, (tok, tok), 1)
    before = jnp.where(older < newer, 1.0, 0.0).astype(BF16)
    hot = jnp.where(one_hot, 1.0, 0.0)
    earlier = jnp.dot(hot.astype(BF16), before, preferred_element_type=F32)
    position = jnp.sum(earlier * hot, axis=0, keepdims=True)
    dest = ids_row.astype(F32) * float(cap) + position
    eye = older == newer
    dispatch = []
    for first, rows in batches:
        row = lax.broadcasted_iota(jnp.int32, (rows, tok), 0)
        slot = jnp.concatenate([row + (e * cap + first) for e in range(n_exp)], axis=0).astype(F32)
        dispatch.append(jnp.where(slot == dest, 1.0, 0.0).astype(BF16))
    small[1].wait()
    factor = jnp.sum(jnp.where(eye, jax.nn.sigmoid(logit[...]), 0.0), axis=1, keepdims=True)

    def exchange(b, c, kind):
        _, _, row, rows = plans[b][c]
        src, dst = r["send_" + kind][b], r["recv_" + kind][b]
        copies = []
        for k in order:
            e = lax.rem(g + k, n_exp)
            copies.append(
                pltpu.make_async_remote_copy(
                    src_ref=src.at[e, pl.ds(row, rows)],
                    dst_ref=dst.at[g, pl.ds(row, rows)],
                    send_sem=r["s_" + kind].at[b, c],
                    recv_sem=r["r_" + kind].at[b, c],
                    device_id=(e, t),
                    device_id_type=MESH,
                )
            )
        return copies

    def to_tensor(src, dst, kind, b, c, peer):
        return pltpu.make_async_remote_copy(
            src_ref=src,
            dst_ref=dst,
            send_sem=r["s_" + kind].at[b, c],
            recv_sem=r["r_" + kind].at[b, c],
            device_id=(g, peer),
            device_id_type=MESH,
        )

    def post(b, c, kind, values):
        _, lanes, row, rows = plans[b][c]
        n = batches[b][1]
        src, dst = r["send_" + kind][b], r["recv_" + kind][b]
        for e in range(n_exp):
            src[e, row : row + rows] = pack(values[e * n : (e + 1) * n], lanes, rows).astype(BF16)
        copies = exchange(b, c, kind)
        if kind == "d" and b == 0 and c == 0:
            pl.semaphore_wait(barrier, n_exp - 1 + 2)
        for copy in copies:
            copy.start()
        dst[g, row : row + rows] = src[g, row : row + rows]
        return copies

    def wait_blocks(b, c, kind, side):
        _, _, row, rows = plans[b][c]
        part = r[("send_" if side == "s" else "recv_") + kind][b].at[pl.ds(0, n_exp - 1), pl.ds(row, rows)]
        pltpu.make_async_copy(part, part, r[side + "_" + kind].at[b, c]).wait()

    def collect(b, c, kind):
        _, lanes, row, rows = plans[b][c]
        wait_blocks(b, c, kind, "r")
        src = r["recv_" + kind][b]
        return jnp.concatenate(
            [unpack(src[e, row : row + rows], lanes, batches[b][1]) for e in range(n_exp)], axis=0
        ).astype(BF16)

    small[2].wait()
    for load in w_loads[:4]:
        load.start()
    scaled = (factor * tokens[...].astype(F32)).astype(BF16)
    for b in all_b:
        for c in range(n_chunks):
            off, lanes, _, _ = plans[b][c]
            outgoing = jnp.dot(dispatch[b], scaled[:, off : off + lanes], preferred_element_type=F32)
            post(b, c, "d", outgoing)

    for load in w_loads[4:] + down_loads:
        load.start()

    dest_col = jnp.sum(jnp.where(eye, dest, 0.0), axis=1, keepdims=True)
    for b, (first, rows) in enumerate(batches):
        lane = lax.broadcasted_iota(jnp.int32, (1, n_exp * rows), 1)
        slot = lane + first
        for e in range(1, n_exp):
            slot = slot + jnp.where(lane >= e * rows, cap - rows, 0)
        combine[b][...] = jnp.where(slot.astype(F32) == dest_col, 1.0, 0.0).astype(BF16)

    crossing, sides, forwards = {}, {}, {}

    def gather(b, c):
        off, lanes, _, _ = plans[b][c]
        x = r["x"][b]
        x[t, :, off : off + lanes] = collect(b, c, "d")
        part = x.at[t, :, pl.ds(off, lanes)]
        crossing[b, c] = to_tensor(part, part, "cross", b, c, across)
        sides[b, c] = to_tensor(part, part, "side", b, c, sib)
        crossing[b, c].start()
        sides[b, c].start()

    def forward(b, c):
        off, lanes, _, _ = plans[b][c]
        crossing[b, c].wait_recv()
        part = r["x"][b].at[across, :, pl.ds(off, lanes)]
        forwards[b, c] = to_tensor(part, part, "fwd", b, c, sib)
        forwards[b, c].start()

    def project(b, c, one, two, begin, end):
        off, lanes, _, _ = plans[b][c]
        x, acc_g, acc_u, hidden = r["x"][b], r["acc_g"][b], r["acc_u"][b], r["hidden"][b]
        feats = slice(off, off + lanes)
        rows_in = jnp.concatenate([x[one, :, feats], x[two, :, feats]], axis=1)
        for n in range(0, n_ff, tile):
            cols = slice(n, n + tile)

            def product(w):
                w_in = jnp.concatenate([w[one, feats, cols], w[two, feats, cols]], axis=0)
                return jnp.dot(rows_in, w_in, preferred_element_type=F32)

            gate, lift = product(wg), product(wu)
            if not begin:
                gate = gate + acc_g[:, cols]
                lift = lift + acc_u[:, cols]
            if end:
                hidden[:, cols] = ((0.5 * gate) * (1.0 + jnp.tanh(0.5 * gate)) * lift).astype(BF16)
            else:
                acc_g[:, cols] = gate
                acc_u[:, cols] = lift

    def near_pair(b, c):
        sides[b, c].wait_recv()
        project(b, c, t, sib, c == 0, False)

    def far_pair(b, c):
        forwards[b, c].wait_recv()
        project(b, c, across, diag, False, c == n_chunks - 1)

    back = list(range(n_chunks))[::-1]
    fars, halves, nears = {}, {}, {}

    def partials(b, one, two, c):
        off, lanes, _, _ = plans[b][c]
        rows_in, part = r["hidden"][b][...], slice(off, off + lanes)
        if lanes == 128:
            both = jnp.dot(
                rows_in,
                jnp.concatenate([wd[one, :, part], wd[two, :, part]], axis=1),
                preferred_element_type=F32,
            )
            return (lambda: both[:, :lanes]), (lambda: both[:, lanes:])
        return tuple(
            functools.partial(jnp.dot, rows_in, wd[s, :, part], preferred_element_type=F32) for s in (one, two)
        )

    def start_far(b, c):
        off, lanes, _, _ = plans[b][c]
        part = pl.ds(off, lanes)
        theirs, mine = partials(b, diag, across, c)
        r["far_out"][b][:, off : off + lanes] = theirs()
        fars[b, c] = to_tensor(r["far_out"][b].at[:, part], r["far_in"][b].at[:, part], "far", b, c, sib)
        fars[b, c].start()
        r["far_own"][b][:, off : off + lanes] = mine()

    def start_half(b, c):
        off, lanes, _, _ = plans[b][c]
        part, lane = pl.ds(off, lanes), slice(off, off + lanes)
        fars[b, c].wait_recv()
        r["half_out"][b][:, lane] = (r["far_own"][b][:, lane] + r["far_in"][b][:, lane]).astype(BF16)
        halves[b, c] = to_tensor(r["half_out"][b].at[:, part], r["half_in"][b].at[:, part], "half", b, c, across)
        halves[b, c].start()

    def far_side(b):
        start_far(b, back[0])
        for i, c in enumerate(back):
            if i + 1 < n_chunks:
                start_far(b, back[i + 1])
            start_half(b, c)

    def near_side(b):
        for c in back:
            off, lanes, _, _ = plans[b][c]
            part = pl.ds(off, lanes)
            theirs, mine = partials(b, sib, t, c)
            r["near_out"][b][:, off : off + lanes] = theirs()
            nears[b, c] = to_tensor(r["near_out"][b].at[:, part], r["near_in"][b].at[:, part], "near", b, c, sib)
            nears[b, c].start()
            r["near_own"][b][:, off : off + lanes] = mine()

    def give_back(b, c):
        off, lanes, _, _ = plans[b][c]
        lane = slice(off, off + lanes)
        nears[b, c].wait_recv()
        halves[b, c].wait_recv()
        total = (
            r["near_own"][b][:, lane] + r["near_in"][b][:, lane] + r["half_in"][b][:, lane].astype(F32)
        )
        post(b, c, "r", total)

    last = n_chunks - 1

    gather(0, 0)
    for load in w_loads[:4]:
        load.wait()
    near_pair(0, 0)
    for c in range(1, n_chunks):
        gather(0, c)
        if c == 1:
            forward(0, 0)
        if c < last:
            near_pair(0, c)
    for load in w_loads[4:]:
        load.wait()
    far_pair(0, 0)
    for c in range(1, last):
        forward(0, c)
    near_pair(0, last)
    forward(0, last)
    for c in range(1, n_chunks):
        far_pair(0, c)
    for load in down_loads:
        load.wait()
    far_side(0)
    near_side(0)
    for c in range(n_chunks):
        wait_blocks(0, c, "d", "s")
    for group in (crossing, sides, forwards, fars):
        for copy in group.values():
            copy.wait_send()
    for c in back:
        give_back(0, c)
    for group in (halves, nears):
        for copy in group.values():
            copy.wait_send()

    for c in back:
        off, lanes, _, _ = plans[0][c]
        mixed = None
        for b in all_b:
            term = jnp.dot(combine[b][...], collect(b, c, "r"), preferred_element_type=F32)
            mixed = term if mixed is None else mixed + term
        out[:, off : off + lanes] = mixed.astype(BF16)

    for c in back:
        wait_blocks(0, c, "r", "s")


def grouped(n_b, single, per_batch, n_exp, n_ten, cap, batches, plans, *refs):
    refs = list(refs)
    names, values = [], []
    for name in single:
        names.append(name)
        values.append(refs.pop(0))
    for name in per_batch:
        names.append(name)
        values.append([refs.pop(0) for _ in range(n_b)])
    kernel(n_exp, n_ten, cap, batches, plans, names, *values)


def fused(tokens, route_logit, expert_ids, w_gate, w_up, w_down):
    n_exp = lax.axis_size("expert")
    n_ten = lax.axis_size("tensor")
    tok, width = tokens.shape
    n_ff = w_gate.shape[2]
    cap = 5 * tok // (4 * n_exp)
    slots = n_exp * cap
    batches = cut(cap)
    made = [plan(width, rows) for _, rows in batches]
    plans = [chunks for chunks, _ in made]
    n_b, n_c = len(batches), len(plans[0])
    vmem, dma = pltpu.VMEM, pltpu.SemaphoreType.DMA
    scratch = {
        "tokens": vmem((tok, width), BF16),
        "logit": vmem((1, tok), F32),
        "ids": vmem((1, tok), jnp.int32),
        "wg": vmem((n_ten, width, n_ff), BF16),
        "wu": vmem((n_ten, width, n_ff), BF16),
        "wd": vmem((n_ten, n_ff, width), BF16),
        "in_sem": dma((3,)),
        "w_sem": dma((3, n_ten)),
    }
    for kind in ("d", "r"):
        scratch["s_" + kind] = dma((n_b, n_c))
        scratch["r_" + kind] = dma((n_b, n_c))
    for kind in ("cross", "side", "fwd", "far", "half", "near"):
        scratch["s_" + kind] = dma((n_b, n_c))
        scratch["r_" + kind] = dma((n_b, n_c))
    lists = {}
    for name in ("send_d", "recv_d", "send_r", "recv_r"):
        lists[name] = [vmem((n_exp, block, 128), BF16) for _, block in made]
    counts = [n_exp * rows for _, rows in batches]
    lists["x"] = [vmem((n_ten, n, width), BF16) for n in counts]
    for name in ("acc_g", "acc_u"):
        lists[name] = [vmem((n, n_ff), F32) for n in counts]
    lists["hidden"] = [vmem((n, n_ff), BF16) for n in counts]
    lists["combine"] = [vmem((tok, n), BF16) for n in counts]
    for name in ("far_out", "far_in", "far_own", "near_out", "near_in", "near_own"):
        lists[name] = [vmem((n, width), F32) for n in counts]
    for name in ("half_out", "half_in"):
        lists[name] = [vmem((n, width), BF16) for n in counts]
    single = ["tokens_in", "logit_in", "ids_in", "w_gate", "w_up", "w_down", "out"] + list(scratch)
    return pl.pallas_call(
        functools.partial(grouped, n_b, single, list(lists), n_exp, n_ten, cap, batches, plans),
        out_shape=jax.ShapeDtypeStruct((tok, width), BF16),
        in_specs=[pl.BlockSpec(memory_space=pl.ANY)] * 6,
        out_specs=pl.BlockSpec(memory_space=vmem),
        scratch_shapes=list(scratch.values()) + [ref for group in lists.values() for ref in group],
        compiler_params=pltpu.CompilerParams(
            collective_id=0, has_side_effects=True, vmem_limit_bytes=LIMIT
        ),
        cost_estimate=pl.CostEstimate(
            flops=6 * slots * n_ten * width * n_ff,
            bytes_accessed=6 * n_ten * width * n_ff,
            transcendentals=slots * n_ff,
        ),
    )(tokens, route_logit.reshape(1, tok), expert_ids.reshape(1, tok), w_gate, w_up, w_down)


def on_device(tokens, route_logit, expert_ids, w_gate, w_up, w_down):
    expert_count = lax.axis_size("expert")
    tok_rows, width_local = tokens.shape
    capacity = 5 * tok_rows // (4 * expert_count)
    if (
        lax.axis_size("tensor") == 4
        and capacity % 8 == 0
        and width_local % 128 == 0
        and w_gate.shape[2] % 256 == 0
        and expert_count <= 8
    ):
        return fused(tokens, route_logit, expert_ids, w_gate, w_up, w_down)
    slot_count = expert_count * capacity
    route = expert_ids[:, 0]
    one_hot = (route[:, None] == jnp.arange(expert_count, dtype=jnp.int32)[None, :]).astype(
        jnp.int32
    )
    earlier = jnp.cumsum(one_hot, axis=0) - one_hot
    position = jnp.sum(earlier * one_hot, axis=1)
    destination = route * capacity + position
    dispatch_map = (
        jnp.arange(slot_count, dtype=jnp.int32)[:, None] == destination[None, :]
    ).astype(jnp.bfloat16)
    factor = jax.nn.sigmoid(route_logit)
    scaled = (factor[:, None] * tokens.astype(jnp.float32)).astype(jnp.bfloat16)
    outgoing = jnp.dot(dispatch_map, scaled, preferred_element_type=jnp.float32).astype(
        jnp.bfloat16
    )
    outgoing = outgoing.reshape(expert_count, capacity, width_local)
    arrived = lax.all_to_all(outgoing, "expert", split_axis=0, concat_axis=0, tiled=True).reshape(
        slot_count, width_local
    )
    gate_local = w_gate[0]
    lift_local = w_up[0]
    down_local = w_down[0]
    piece = lax.all_gather(arrived, "tensor", axis=1, tiled=True)
    gate_val = jnp.dot(piece, gate_local, preferred_element_type=jnp.float32)
    lift_val = jnp.dot(piece, lift_local, preferred_element_type=jnp.float32)
    hidden = (jax.nn.silu(gate_val) * lift_val).astype(jnp.bfloat16)
    summed = lax.psum_scatter(
        lax.dot_general(
            down_local, hidden, (((0,), (1,)), ((), ())), preferred_element_type=jnp.float32
        ),
        "tensor",
        scatter_dimension=0,
        tiled=True,
    )
    expert_out = summed.astype(jnp.bfloat16).reshape(width_local, expert_count, capacity)
    returned = lax.all_to_all(
        expert_out, "expert", split_axis=1, concat_axis=1, tiled=True
    ).reshape(width_local, slot_count)
    mixed = lax.dot_general(
        dispatch_map, returned, (((0,), (1,)), ((), ())), preferred_element_type=jnp.float32
    )
    return mixed.astype(jnp.bfloat16)


def solution(mesh):
    return jax.shard_map(
        on_device,
        mesh=mesh,
        in_specs=(
            P("expert", "tensor"),
            P("expert"),
            P("expert", None),
            P("expert", None, "tensor"),
            P("expert", None, "tensor"),
            P("expert", "tensor", None),
        ),
        out_specs=P("expert", "tensor"),
        check_vma=False,
    )
```
